256 devices in a mesh: panel: 64 (over y, x, z_lo), slab: 4 (over z_hi, core).
Axes of the slice: x: 4, y: 4, z: 8 (z_hi: 2, z_lo: 4; z = z_hi * 4 + z_lo), core: 2. Of those that a mesh axis runs over, the one named last changes fastest.
Arguments:
- clip_cache: float32 [1024, 8192], P(None, 'panel'), may hold values from -6 to 6
- dose_scale: float32 [16, 8192], P(None, 'panel'), may hold values from 0.3 to 3
- focus_term: float32 [8, 8192], P(None, 'panel'), may hold values from -3 to 3
- clip_ids: int32 [32768], P('slab'), may hold values from 0 to 1023
- dose_ids: int32 [32768], P('slab'), may hold values from 0 to 15
- focus_ids: int32 [32768], P('slab'), may hold values from 0 to 7
Outputs:
- rotated: float32 [32768, 8192], P('slab', 'panel')
The draws below stay inside these ranges and needn't reach their ends.
All inputs are finite; a program needn't handle non-finite values.
Results may differ from the reference program's by a relative error of at most 0.0001.
Values sent between devices are 32-bit elements; how exact they have to be, the bound alone decides.
A program may use at most 64 MiB of HBM per device.

```python
import math
import jax
import jax.numpy as jnp
from jax import lax

PANEL_COLS = 128
ROUNDS = 2
NCLIP = 1024
NDOSE = 16
NFOCUS = 8
M = 32768
NCOL = 8192
N_PANEL = 64


def plant(values, own_key, low, largest):
    place = [jax.random.randint(jax.random.fold_in(own_key, axis), (), 0, length) for axis, length in enumerate(values.shape)]
    longest = values.shape.index(max(values.shape))
    neighbour = place[:longest] + [(place[longest] + 1) % values.shape[longest]] + place[longest + 1:]
    return values.at[tuple(place)].set(low).at[tuple(neighbour)].set(largest)


def steps_of(stream_key, dims, cuts, least, top_value):
    def one(position, blocks):
        heights = jax.random.uniform(jax.random.fold_in(jax.random.fold_in(stream_key, 6), position), (blocks,), jnp.float32, least / len(cuts), top_value / len(cuts))
        return jnp.repeat(jnp.exp(heights), dims[position] // blocks).reshape((-1,) + (1,) * (len(dims) - position - 1))

    gain = one(*cuts[0])
    for cut in cuts[1:]:
        gain = gain * one(*cut)
    return gain


def normal_values(key, extent, scale, bound, cuts=(), kind=jnp.bfloat16):
    entries = scale * jax.random.normal(key, extent, jnp.float32)
    if cuts:
        entries = entries * steps_of(key, extent, cuts, -0.22, 0.18)
    return jnp.clip(entries, -bound, bound).astype(kind)


def setup_inputs(seed: int = 0) -> dict:
    splits = jax.random.split(jax.random.key(seed), 7)
    clip_cache = normal_values(splits[0], (NCLIP, NCOL), 1.0, 6.0, ((1, 64),), jnp.float32)
    dose_scale = jnp.clip(jnp.exp(math.log(3.0) - 2.3025851 * jax.random.uniform(splits[1], (NDOSE, NCOL), jnp.float32) ** steps_of(splits[1], (NDOSE, NCOL), ((1, 64),), -0.2, 0.2)), 0.3, 3.0)
    focus_term = normal_values(splits[2], (NFOCUS, NCOL), 0.5, 3.0, ((1, 64),), jnp.float32)
    clip_ids = plant(jax.random.randint(splits[3], (M,), 0, NCLIP), jax.random.fold_in(splits[3], 1), 0, NCLIP - 1).astype(jnp.int32)
    dose_ids = plant(jax.random.randint(splits[4], (M,), 0, NDOSE), jax.random.fold_in(splits[4], 1), 0, NDOSE - 1).astype(jnp.int32)
    focus_ids = plant(jax.random.randint(splits[5], (M,), 0, NFOCUS), jax.random.fold_in(splits[5], 1), 0, NFOCUS - 1).astype(jnp.int32)
    return dict(clip_cache=clip_cache, dose_scale=dose_scale, focus_term=focus_term, clip_ids=clip_ids, dose_ids=dose_ids, focus_ids=focus_ids)


EPSILON = 1e-06

def block_rotation(gram):
    doubled = gram.shape[0]
    half_size = doubled // 2
    diagonal = jnp.diagonal(gram)
    coupling = gram / (diagonal[:, None] + diagonal[None, :])
    positions = lax.iota(jnp.int32, doubled)
    upper_mask = (positions[:, None] < half_size) & (positions[None, :] >= half_size)
    lower_mask = (positions[:, None] >= half_size) & (positions[None, :] < half_size)
    generator = 0.5 * (jnp.where(upper_mask, coupling, 0.0) - jnp.where(lower_mask, coupling, 0.0))
    identity = jnp.eye(doubled, dtype=gram.dtype)
    plus_half = identity + generator
    symmetric = identity + jnp.dot(generator.T.astype(jnp.float32), generator.astype(jnp.float32), precision=lax.Precision.HIGHEST, preferred_element_type=jnp.float32)
    factor = jnp.linalg.cholesky(symmetric)
    numerator = jnp.dot(plus_half.astype(jnp.float32), plus_half.astype(jnp.float32), precision=lax.Precision.HIGHEST, preferred_element_type=jnp.float32)
    return jax.scipy.linalg.cho_solve((factor, True), numerator)

def rotate_pair(pair):
    left_panel, right_panel = pair
    panel_width = left_panel.shape[1]
    pair_block = jnp.concatenate([left_panel, right_panel], axis=1)
    gram = lax.dot_general(pair_block.astype(jnp.float32), pair_block.astype(jnp.float32), (((0,), (0,)), ((), ())), precision=lax.Precision.HIGHEST, preferred_element_type=jnp.float32)
    rotated = jnp.dot(pair_block.astype(jnp.float32), block_rotation(gram).astype(jnp.float32), precision=lax.Precision.HIGHEST, preferred_element_type=jnp.float32)
    return (rotated[:, :panel_width], rotated[:, panel_width:])

def reference(clip_cache, dose_scale, focus_term, clip_ids, dose_ids, focus_ids):
    jacobian = clip_cache[clip_ids] * dose_scale[dose_ids] + focus_term[focus_ids]
    col_squares = lax.optimization_barrier(jnp.sum(jacobian * jacobian, axis=0))
    jacobian = jacobian * (1.0 / jnp.sqrt(col_squares / M + EPSILON))
    panels = jacobian.reshape(M, N_PANEL, PANEL_COLS).transpose(1, 0, 2)
    evens = panels[0::2]
    odds = panels[1::2]
    for section in range(ROUNDS):
        if section > 0:
            seats = jnp.stack([evens, odds], axis=1).reshape(N_PANEL, M, PANEL_COLS)
            seats = jnp.roll(seats, 1, axis=0)
            evens = seats[0::2]
            odds = seats[1::2]
        evens, odds = lax.map(rotate_pair, (evens, odds))
    seats = jnp.stack([evens, odds], axis=1).reshape(N_PANEL, M, PANEL_COLS)
    return seats.transpose(1, 0, 2).reshape(M, N_PANEL * PANEL_COLS)
```

```python
import functools

import jax
import jax.numpy as jnp
from jax import lax
from jax.experimental import pallas as pl
from jax.experimental.pallas import tpu as pltpu
from jax.sharding import PartitionSpec as P

MESH = pl.DeviceIdType.MESH
EPSILON = 1e-06
F32 = jnp.float32
BF16 = jnp.bfloat16
ANY = pl.BlockSpec(memory_space=pl.ANY)
VMEM = pl.BlockSpec(memory_space=pltpu.VMEM)
SMEM = pl.BlockSpec(memory_space=pltpu.SMEM)


def exchange(seats, c_ref, d_ref, f_ref, i_ref, j_ref, k_ref, cs, ds, fs, ci, di, fi, local_sem, send_sem, recv_sem):
    seat = lax.axis_index("panel")
    slab = lax.axis_index("slab")
    z_hi, core = slab // 2, slab % 2
    side = seat % 2
    base = seat - side
    nclip = c_ref.shape[0]
    half = nclip // 2

    def near(target):
        z_lo = target % 4
        other = jnp.where((z_lo == 0) | (z_lo == 3), 1, 0)
        return (z_hi + other) % 2

    partner = (seat + 1 - 2 * side, slab)
    next0 = (base + 2) % seats
    next1 = (base + 3) % seats
    to_next0 = (next0, near(next0) * 2 + core)
    to_next1 = (next1, near(next1) * 2 + core)
    from_group = near(seat) * 2 + core
    from_prev0 = ((base + seats - 2) % seats, from_group)
    from_prev1 = ((base + seats - 1) % seats, from_group)
    z_lo = seat % 4
    mirror = (seat - z_lo + 3 - z_lo, (1 - z_hi) * 2 + core)
    twin = (seat, z_hi * 2 + 1 - core)

    barrier = pltpu.get_barrier_semaphore()
    for device in (partner, from_prev0, from_prev1, mirror, twin):
        pl.semaphore_signal(barrier, inc=1, device_id=device, device_id_type=MESH)
    pl.semaphore_wait(barrier, 5)

    def remote(number, source, target, device, arrival=None):
        return pltpu.make_async_remote_copy(
            src_ref=source,
            dst_ref=target,
            send_sem=send_sem.at[number],
            recv_sem=recv_sem.at[number if arrival is None else arrival],
            device_id=device,
            device_id_type=MESH,
        )

    mine = pl.ds(pl.multiple_of(core * half, 8), half)
    own = 2 + side
    mate = 3 - side
    ids = (i_ref, ci), (j_ref, di), (k_ref, fi)

    sent = []
    for n, (source, target) in enumerate(ids):
        sent.append(remote(n, source, target.at[1], mirror))
    sent.append(remote(9, c_ref.at[mine], cs.at[own, mine], partner))
    sent.append(remote(12, d_ref, ds.at[own], partner))
    sent.append(remote(15, f_ref, fs.at[own], partner))
    for n, device in enumerate((to_next0, to_next1)):
        sent.append(remote(10 + n, c_ref.at[mine], cs.at[side, mine], device, 10 + side))
        sent.append(remote(13 + n, d_ref, ds.at[side], device, 13 + side))
        sent.append(remote(16 + n, f_ref, fs.at[side], device, 16 + side))
    for n, (source, target) in enumerate(ids):
        sent.append(remote(3 + n, source, target.at[2], twin))
    for copy in sent:
        copy.start()
    local = [
        pltpu.make_async_copy(c_ref, cs.at[own], local_sem.at[0]),
        pltpu.make_async_copy(d_ref, ds.at[own], local_sem.at[1]),
        pltpu.make_async_copy(f_ref, fs.at[own], local_sem.at[2]),
    ]
    for n, (source, target) in enumerate(ids):
        local.append(pltpu.make_async_copy(source, target.at[0], local_sem.at[3 + n]))
    for copy in local:
        copy.start()

    for n, (source, target) in enumerate(ids):
        remote(n, source, target.at[1], mirror).wait_recv()
        forward = remote(6 + n, target.at[1], target.at[3], twin)
        forward.start()
        sent.append(forward)
    for n, slot in ((9, mate), (10, 0), (11, 1)):
        remote(n, c_ref.at[mine], cs.at[slot, mine], partner).wait_recv()
        forward = remote(9 + n, cs.at[slot, mine], cs.at[slot, mine], twin)
        forward.start()
        sent.append(forward)
    for n, slot in ((12, mate), (13, 0), (14, 1)):
        remote(n, d_ref, ds.at[slot], partner).wait_recv()
        remote(n + 3, f_ref, fs.at[slot], partner).wait_recv()
    for n, (source, target) in enumerate(ids):
        remote(3 + n, source, target.at[2], twin).wait_recv()
        remote(6 + n, source, target.at[3], twin).wait_recv()
    theirs = pl.ds(pl.multiple_of((1 - core) * half, 8), half)
    for n, slot in ((18, mate), (19, 0), (20, 1)):
        remote(n, c_ref.at[theirs], cs.at[slot, theirs], twin).wait_recv()
    for copy in sent:
        copy.wait_send()
    for copy in local:
        copy.wait()


def gather_tables(seats, clip_cache, dose_scale, focus_term, ids):
    rows, cols = ids[0].shape
    out = [
        jax.ShapeDtypeStruct((4, *clip_cache.shape), F32),
        jax.ShapeDtypeStruct((4, *dose_scale.shape), F32),
        jax.ShapeDtypeStruct((4, *focus_term.shape), F32),
    ] + [jax.ShapeDtypeStruct((4, rows, cols), jnp.int32)] * 3
    return pl.pallas_call(
        functools.partial(exchange, seats),
        out_shape=out,
        in_specs=[ANY] * 6,
        out_specs=[ANY] * 6,
        scratch_shapes=[
            pltpu.SemaphoreType.DMA((6,)),
            pltpu.SemaphoreType.DMA((21,)),
            pltpu.SemaphoreType.DMA((21,)),
        ],
        compiler_params=pltpu.CompilerParams(collective_id=0, has_side_effects=True),
        name="exchange",
    )(clip_cache, dose_scale, focus_term, *ids)


def split(value):
    high = value.astype(BF16)
    return high, (value - high.astype(F32)).astype(BF16)


def dot(a, b, dims=((1,), (0,))):
    return lax.dot_general(a, b, (dims, ((), ())), preferred_element_type=F32)


def three(value):
    high = value.astype(BF16)
    rest = value - high.astype(F32)
    middle = rest.astype(BF16)
    return high, middle, (rest - middle.astype(F32)).astype(BF16)


def full(a, b, dims=((1,), (0,))):
    a1, a2, a3 = three(a)
    b1, b2, b3 = three(b)
    small = dot(a2, b2, dims) + dot(a1, b3, dims) + dot(a3, b1, dims)
    return dot(a1, b1, dims) + (dot(a1, b2, dims) + dot(a2, b1, dims) + small)


TN = ((0,), (0,))
NT = ((1,), (1,))


def column(row):
    return jnp.broadcast_to(row, (128, row.shape[1])).T[:, :1]


def inverses(bs, state):
    n = bs[0].shape[0]
    eye = (lax.broadcasted_iota(jnp.int32, (n, n), 0) == lax.broadcasted_iota(jnp.int32, (n, n), 1)).astype(F32)
    squares = [full(b, b, NT) for b in bs]
    bound = functools.reduce(jnp.maximum, [jnp.max(jnp.sum(jnp.abs(s), axis=1)) for s in squares])
    scale = 2.0 / (2.0 + bound)
    for e, s in enumerate(squares):
        rest = (1.0 - scale) * eye - scale * s
        state[e, :n, :] = scale * (eye + rest)
        state[e, n:, :] = full(rest, rest)
    ratio = bound / (2.0 + bound)

    def body(ratio):
        for e in range(len(bs)):
            old = state[e]
            new = full(old, old[n:])
            state[e, :n, :] = old[:n] + new[:n]
            state[e, n:, :] = new[n:]
        return ratio * ratio

    lax.while_loop(lambda ratio: ratio > 1e-8, body, ratio * ratio)
    return [state[e, :n, :] for e in range(len(bs))], eye


def compute(
    total, cs, ds, fs, ci, di, fi, clip_ids, dose_ids, focus_ids, out,
    ch, cl, ct, counts, drow, dcol, gram, table, fw, wd, state,
):
    nclip, width = cs.shape[1:]
    ndose, nfocus = ds.shape[1], fs.shape[1]
    cols = 4 * width
    for p in range(4):
        high, low = split(cs[p])
        lanes = pl.ds(p * width, width)
        ch[:, lanes] = high
        cl[:, lanes] = low
        ct[lanes, :] = cs[p].T
        drow[:, lanes] = ds[p]
        dcol[lanes, :] = jnp.concatenate([ds[p], jnp.zeros((128 - ndose, width), F32)], axis=0).T

    counts[...] = jnp.zeros_like(counts)
    tall = lax.broadcasted_iota(jnp.int32, (512, 128), 0)
    wide = lax.broadcasted_iota(jnp.int32, (256, 128), 0)
    step_rows = 8

    def count(step, _):
        slab = step // (ci.shape[1] // step_rows)
        rows = pl.ds(pl.multiple_of(step % (ci.shape[1] // step_rows) * step_rows, step_rows), step_rows)
        clip = ci[slab, rows, :]
        first = (clip // 256) * 128 + di[slab, rows, :] * nfocus + fi[slab, rows, :]
        second = clip % 256
        a = jnp.concatenate([(tall == first[r : r + 1, :]).astype(F32).astype(BF16) for r in range(step_rows)], axis=1)
        b = jnp.concatenate([(wide == second[r : r + 1, :]).astype(F32).astype(BF16) for r in range(step_rows)], axis=1)
        counts[...] += dot(a, b, NT)
        return 0

    lax.fori_loop(0, 4 * ci.shape[1] // step_rows, count, 0)

    n = jnp.concatenate([counts[h * 128 : (h + 1) * 128, :] for h in range(4)], axis=1)
    fall = jnp.concatenate([fs[p] for p in range(4)], axis=1)
    nh, nl = split(n)
    v = dot(nh, ch[...]) + dot(nh, cl[...]) + dot(nl, ch[...])
    s = jnp.zeros((nfocus, cols), F32)
    per_focus = jnp.zeros((nfocus, nclip), F32)
    for j in range(ndose):
        s = s + v[j * nfocus : (j + 1) * nfocus, :] * drow[j : j + 1, :]
        per_focus = per_focus + n[j * nfocus : (j + 1) * nfocus, :]
    nk = jnp.sum(per_focus, axis=1, keepdims=True)
    s = s + 0.5 * nk * fall
    gram[...] = full(jnp.concatenate([s, fall], axis=0), jnp.concatenate([fall, s], axis=0), TN)

    lane = lax.broadcasted_iota(jnp.int32, (cols, 128), 1)

    def dose(j, _):
        begin = pl.multiple_of(j * nfocus, nfocus)
        nj = jnp.concatenate(
            [jnp.sum(counts[pl.ds(h * 128 + begin, nfocus), :], axis=0, keepdims=True) for h in range(4)], axis=1
        )
        dj = jnp.sum(jnp.where(lane == j, dcol[...], 0.0), axis=1, keepdims=True)
        row = drow[pl.ds(j, 1), :]
        for m in range(2):
            here = pl.ds(m * 256, 256)
            right = pl.ds(m * 256, cols - m * 256)
            uh, ul = split(ct[here, :] * nj * dj[m * 256 : (m + 1) * 256, :])
            part = dot(uh, ch[:, right]) + dot(uh, cl[:, right]) + dot(ul, ch[:, right])
            gram[here, right] += part * row[:, m * 256 :]
        return 0

    lax.fori_loop(0, ndose, dose, 0)

    row_i = lax.broadcasted_iota(jnp.int32, (128, 128), 0)
    col_i = lax.broadcasted_iota(jnp.int32, (128, 128), 1)
    squares = jnp.concatenate(
        [
            jnp.sum(jnp.where(row_i == col_i, gram[p * 128 : (p + 1) * 128, p * 128 : (p + 1) * 128], 0.0), axis=0, keepdims=True)
            for p in range(4)
        ],
        axis=1,
    )
    inverse_norm = 1.0 / jnp.sqrt(squares / total + EPSILON)
    norm_col = column(inverse_norm)
    d = squares * inverse_norm * inverse_norm
    d_col = column(d)
    g_prev = gram[:256, :256] * norm_col[:256] * inverse_norm[:, :256]
    g_cross = gram[:256, 256:] * norm_col[:256] * inverse_norm[:, 256:]
    g_own = gram[256:, 256:] * norm_col[256:] * inverse_norm[:, 256:]
    b_prev = 0.5 * g_prev[:128, 128:] / (d_col[:128] + d[:, 128:256])
    b_own = 0.5 * g_own[:128, 128:] / (d_col[256:384] + d[:, 384:])
    (m_prev, m_own), eye = inverses([b_prev, b_own], state)
    z = 2.0 * full(m_prev, b_prev)
    q_right = jnp.concatenate([z, eye - full(b_prev, z, TN)], axis=0)
    q_left = jnp.concatenate([2.0 * m_own - eye, -2.0 * full(b_own, m_own, TN)], axis=0)

    cross = full(full(q_right, g_cross, TN), q_left)
    d_left = jnp.sum(q_right * full(g_prev, q_right), axis=0, keepdims=True)
    d_right = jnp.sum(q_left * full(g_own, q_left), axis=0, keepdims=True)
    b = 0.5 * cross / (column(d_left) + d_right)
    (m,), _ = inverses([b], state)
    z = 2.0 * full(m, b)
    odd = lax.axis_index("panel") % 2 == 1
    top = jnp.where(odd, z, 2.0 * m - eye)
    bottom = jnp.where(odd, eye - full(b, z, TN), -2.0 * full(b, m, TN))
    w = jnp.concatenate([full(q_right, top), full(q_left, bottom)], axis=0) * norm_col
    fw[...] = full(fall, w)

    wd[...] = w

    def rows_of(pair, _):
        parts = []
        for e in range(2):
            dj = jnp.sum(jnp.where(lane == pair * 2 + e, dcol[...], 0.0), axis=1, keepdims=True)
            parts.append(wd[...] * dj)
        wh, wl = split(jnp.concatenate(parts, axis=1))
        for m in range(nclip // 256):
            here = pl.ds(m * 256, 256)
            part = dot(ch[here, :], wh) + dot(cl[here, :], wh) + dot(ch[here, :], wl)
            for e in range(2):
                begin = pl.multiple_of((pair * 2 + e) * nclip + m * 256, 256)
                table[pl.ds(begin, 256), :] = part[:, e * 128 : (e + 1) * 128]
        return 0

    lax.fori_loop(0, ndose // 2, rows_of, 0)

    unroll = 16

    def gather(step, _):
        begin = pl.multiple_of(step * unroll, unroll)
        for u in range(unroll):
            r = begin + u
            where = dose_ids[r] * nclip + clip_ids[r]
            out[pl.ds(r, 1), :] = table[pl.ds(where, 1), :] + fw[pl.ds(focus_ids[r], 1), :]
        return 0

    lax.fori_loop(0, out.shape[0] // unroll, gather, 0)


def shards(clip_cache, dose_scale, focus_term, clip_ids, dose_ids, focus_ids):
    seats = lax.axis_size("panel")
    rows = clip_ids.shape[0]
    nclip, width = clip_cache.shape
    ndose = dose_scale.shape[0]
    ids = [a.reshape(rows // 128, 128) for a in (clip_ids, dose_ids, focus_ids)]
    gathered = gather_tables(seats, clip_cache, dose_scale, focus_term, ids)
    cols = 4 * width
    return pl.pallas_call(
        functools.partial(compute, float(rows * lax.axis_size("slab"))),
        out_shape=jax.ShapeDtypeStruct((rows, width), F32),
        in_specs=[VMEM] * 6 + [SMEM] * 3,
        out_specs=VMEM,
        scratch_shapes=[
            pltpu.VMEM((nclip, cols), BF16),
            pltpu.VMEM((nclip, cols), BF16),
            pltpu.VMEM((cols, nclip), F32),
            pltpu.VMEM((512, 256), F32),
            pltpu.VMEM((ndose, cols), F32),
            pltpu.VMEM((cols, 128), F32),
            pltpu.VMEM((cols, cols), F32),
            pltpu.VMEM((ndose * nclip, width), F32),
            pltpu.VMEM((focus_term.shape[0], width), F32),
            pltpu.VMEM((cols, width), F32),
            pltpu.VMEM((2, 2 * width, width), F32),
        ],
        compiler_params=pltpu.CompilerParams(vmem_limit_bytes=48 * 2**20),
        name="compute",
    )(*gathered, clip_ids, dose_ids, focus_ids)


def solution(mesh):
    return jax.shard_map(
        shards,
        mesh=mesh,
        in_specs=(
            P(None, "panel"),
            P(None, "panel"),
            P(None, "panel"),
            P("slab"),
            P("slab"),
            P("slab"),
        ),
        out_specs=P("slab", "panel"),
        check_vma=False,
    )
```

```python
import functools

import jax
import jax.numpy as jnp
from jax import lax
from jax.experimental import pallas as pl
from jax.experimental.pallas import tpu as pltpu
from jax.sharding import PartitionSpec as P

MESH = pl.DeviceIdType.MESH
EPSILON = 1e-06
F32 = jnp.float32
BF16 = jnp.bfloat16
ANY = pl.BlockSpec(memory_space=pl.ANY)
VMEM = pl.BlockSpec(memory_space=pltpu.VMEM)


def split(value):
    high = value.astype(BF16)
    return high, (value - high.astype(F32)).astype(BF16)


def dot(a, b, dims=((1,), (0,))):
    return lax.dot_general(a, b, (dims, ((), ())), preferred_element_type=F32)


def three(value):
    high = value.astype(BF16)
    rest = value - high.astype(F32)
    middle = rest.astype(BF16)
    return high, middle, (rest - middle.astype(F32)).astype(BF16)


def full(a, b, dims=((1,), (0,))):
    a1, a2, a3 = three(a)
    b1, b2, b3 = three(b)
    small = dot(a2, b2, dims) + dot(a1, b3, dims) + dot(a3, b1, dims)
    return dot(a1, b1, dims) + (dot(a1, b2, dims) + dot(a2, b1, dims) + small)


TN = ((0,), (0,))
NT = ((1,), (1,))


def column(row):
    return jnp.broadcast_to(row, (128, row.shape[1])).T[:, :1]


def inverses(bs, state):
    n = bs[0].shape[0]
    eye = (lax.broadcasted_iota(jnp.int32, (n, n), 0) == lax.broadcasted_iota(jnp.int32, (n, n), 1)).astype(F32)
    squares = [full(b, b, NT) for b in bs]
    bound = functools.reduce(jnp.maximum, [jnp.max(jnp.sum(jnp.abs(s), axis=1)) for s in squares])
    scale = 2.0 / (2.0 + bound)
    for e, s in enumerate(squares):
        rest = (1.0 - scale) * eye - scale * s
        state[e, :n, :] = scale * (eye + rest)
        state[e, n:, :] = full(rest, rest)
    ratio = bound / (2.0 + bound)

    def body(ratio):
        for e in range(len(bs)):
            old = state[e]
            new = full(old, old[n:])
            state[e, :n, :] = old[:n] + new[:n]
            state[e, n:, :] = new[n:]
        return ratio * ratio

    lax.while_loop(lambda ratio: ratio > 1e-8, body, ratio * ratio)
    return [state[e, :n, :] for e in range(len(bs))], eye


def onehot(places, count, offset):
    value = jnp.broadcast_to(places.astype(F32) - offset, (16, places.shape[1])).astype(BF16)
    tile = lax.broadcasted_iota(jnp.int32, (16, places.shape[1]), 0).astype(F32)
    one, none = jnp.ones_like(value), jnp.zeros_like(value)
    return [jnp.where((tile + 16.0 * t).astype(BF16) == value, one, none) for t in range(count // 16)]


def count_ids(counts, clips, doses, focuses):
    rows = 8

    def count(step, _):
        here = pl.ds(pl.multiple_of(step * rows, rows), rows)
        clip = clips[here, :]
        first = (clip // 256) * 128 + doses[here, :] * 8 + focuses[here, :]
        second = clip % 256
        tall, wide = [], []
        for r in range(rows):
            row = first[r : r + 1, :]
            tall.append(jnp.concatenate(onehot(row, 256, 0.0) + onehot(row, 256, 256.0), axis=0))
            wide.append(jnp.concatenate(onehot(second[r : r + 1, :], 256, 0.0), axis=0))
        counts[...] += dot(jnp.concatenate(tall, axis=1), jnp.concatenate(wide, axis=1), NT)
        return 0

    lax.fori_loop(0, clips.shape[0] // rows, count, 0)


def exchange(
    seats, c_ref, d_ref, f_ref, i_ref, j_ref, k_ref, ch_out, cl_out, ds_out, fs_out, gram_out,
    cs, ds, fs, ci, di, fi, counts, counts_twin, ch, cl, ct, drow, dcol, gram, gram_twin, send_sem, recv_sem, out_sem,
):
    seat = lax.axis_index("panel")
    slab = lax.axis_index("slab")
    z_hi, core = slab // 2, slab % 2
    side = seat % 2
    base = seat - side
    nclip, width = c_ref.shape
    ndose, nfocus = d_ref.shape[0], f_ref.shape[0]
    cols = 4 * width
    half = nclip // 2

    def near(target):
        z_lo = target % 4
        other = jnp.where((z_lo == 0) | (z_lo == 3), 1, 0)
        return (z_hi + other) % 2

    partner = (seat + 1 - 2 * side, slab)
    next0 = (base + 2) % seats
    next1 = (base + 3) % seats
    to_next0 = (next0, near(next0) * 2 + core)
    to_next1 = (next1, near(next1) * 2 + core)
    from_group = near(seat) * 2 + core
    from_prev0 = ((base + seats - 2) % seats, from_group)
    from_prev1 = ((base + seats - 1) % seats, from_group)
    z_lo = seat % 4
    mirror = (seat - z_lo + 3 - z_lo, (1 - z_hi) * 2 + core)
    twin = (seat, z_hi * 2 + 1 - core)

    barrier = pltpu.get_barrier_semaphore()
    for device in (partner, from_prev0, from_prev1, mirror, twin):
        pl.semaphore_signal(barrier, inc=1, device_id=device, device_id_type=MESH)
    pl.semaphore_wait(barrier, 5)

    def remote(number, source, target, device, arrival=None):
        return pltpu.make_async_remote_copy(
            src_ref=source,
            dst_ref=target,
            send_sem=send_sem.at[number],
            recv_sem=recv_sem.at[number if arrival is None else arrival],
            device_id=device,
            device_id_type=MESH,
        )

    mine = pl.ds(pl.multiple_of(core * half, 8), half)
    own = 2 + side
    mate = 3 - side
    ids = (i_ref, ci), (j_ref, di), (k_ref, fi)

    sent = []
    for n, (source, target) in enumerate(ids):
        sent.append(remote(n, source, target, mirror))
    for n, device in enumerate((to_next0, to_next1)):
        sent.append(remote(4 + n, c_ref.at[mine], cs.at[side, mine], device, 4 + side))
        sent.append(remote(7 + n, d_ref, ds.at[side], device, 7 + side))
        sent.append(remote(10 + n, f_ref, fs.at[side], device, 10 + side))
    sent.append(remote(3, c_ref.at[mine], cs.at[own, mine], partner))
    sent.append(remote(6, d_ref, ds.at[own], partner))
    sent.append(remote(9, f_ref, fs.at[own], partner))
    for copy in sent:
        copy.start()
    cs[own] = c_ref[...]
    ds[own] = d_ref[...]
    fs[own] = f_ref[...]

    counts[...] = jnp.zeros_like(counts)
    count_ids(counts, i_ref, j_ref, k_ref)
    for n, (source, target) in enumerate(ids):
        remote(n, source, target, mirror).wait_recv()
    count_ids(counts, ci, di, fi)
    swap_counts = remote(15, counts, counts_twin, twin)
    swap_counts.start()

    for n, slot in ((3, mate), (4, 0), (5, 1)):
        remote(n, c_ref.at[mine], cs.at[slot, mine], partner).wait_recv()
        forward = remote(9 + n, cs.at[slot, mine], cs.at[slot, mine], twin)
        forward.start()
        sent.append(forward)
    for n, slot in ((6, mate), (7, 0), (8, 1)):
        remote(n, d_ref, ds.at[slot], partner).wait_recv()
        remote(n + 3, f_ref, fs.at[slot], partner).wait_recv()
    swap_counts.wait()
    counts[...] += counts_twin[...]
    theirs = pl.ds(pl.multiple_of((1 - core) * half, 8), half)
    for n, slot in ((12, mate), (13, 0), (14, 1)):
        remote(n, c_ref.at[theirs], cs.at[slot, theirs], twin).wait_recv()

    for p in range(4):
        high, low = split(cs[p])
        lanes = pl.ds(p * width, width)
        ch[:, lanes] = high
        cl[:, lanes] = low
        ct[lanes, :] = cs[p].T
        drow[:, lanes] = ds[p]
        dcol[lanes, :] = jnp.concatenate([ds[p], jnp.zeros((128 - ndose, width), F32)], axis=0).T
    outs = [
        pltpu.make_async_copy(source, target, out_sem.at[n])
        for n, (source, target) in enumerate(((ch, ch_out), (cl, cl_out), (ds, ds_out), (fs, fs_out)))
    ]
    for out in outs:
        out.start()

    doses = ndose // 2
    first_dose = core * doses
    begin = pl.multiple_of(first_dose * nfocus, doses * nfocus)
    n = jnp.concatenate([counts[pl.ds(h * 128 + begin, doses * nfocus), :] for h in range(4)], axis=1)
    fall = jnp.concatenate([fs[p] for p in range(4)], axis=1)
    nh, nl = split(n)
    v = dot(nh, ch[...]) + dot(nh, cl[...]) + dot(nl, ch[...])
    dose_rows = drow[pl.ds(pl.multiple_of(first_dose, doses), doses), :]
    s = jnp.zeros((nfocus, cols), F32)
    per_focus = jnp.zeros((nfocus, nclip), F32)
    for j in range(doses):
        s = s + v[j * nfocus : (j + 1) * nfocus, :] * dose_rows[j : j + 1, :]
        per_focus = per_focus + n[j * nfocus : (j + 1) * nfocus, :]
    s = s + 0.5 * jnp.sum(per_focus, axis=1, keepdims=True) * fall
    gram[...] = full(jnp.concatenate([s, fall], axis=0), jnp.concatenate([fall, s], axis=0), TN)

    lane = lax.broadcasted_iota(jnp.int32, (256, 128), 1)
    swaps = []
    for m in range(2):
        here = pl.ds(m * 256, 256)
        right = pl.ds(m * 256, cols - m * 256)

        def dose(step, _, m=m, here=here, right=right):
            j = first_dose + step
            at = pl.multiple_of(j * nfocus, nfocus)
            nj = jnp.concatenate(
                [jnp.sum(counts[pl.ds(h * 128 + at, nfocus), :], axis=0, keepdims=True) for h in range(4)], axis=1
            )
            dj = jnp.sum(jnp.where(lane == j, dcol[here, :], 0.0), axis=1, keepdims=True)
            row = drow[pl.ds(j, 1), right]
            uh, ul = split(ct[here, :] * nj * dj)
            part = dot(uh, ch[:, right]) + dot(uh, cl[:, right]) + dot(ul, ch[:, right])
            gram[here, right] += part * row
            return 0

        lax.fori_loop(0, doses, dose, 0)
        swap = remote(16 + m, gram.at[here, right], gram_twin.at[here, right], twin)
        swap.start()
        swaps.append(swap)
    for m, swap in enumerate(swaps):
        swap.wait()
        here = pl.ds(m * 256, 256)
        right = pl.ds(m * 256, cols - m * 256)
        gram[here, right] += gram_twin[here, right]
        out = pltpu.make_async_copy(gram.at[here, right], gram_out.at[here, right], out_sem.at[4 + m])
        out.start()
        outs.append(out)
    for copy in sent:
        copy.wait_send()
    for out in outs:
        out.wait()


def call_exchange(seats, clip_cache, dose_scale, focus_term, ids):
    nclip, width = clip_cache.shape
    ndose, nfocus = dose_scale.shape[0], focus_term.shape[0]
    cols = 4 * width
    out = [((nclip, cols), BF16)] * 2 + [((4, ndose, width), F32), ((4, nfocus, width), F32), ((cols, cols), F32)]
    return pl.pallas_call(
        functools.partial(exchange, seats),
        out_shape=[jax.ShapeDtypeStruct(*o) for o in out],
        in_specs=[VMEM] * 6,
        out_specs=[ANY] * 5,
        scratch_shapes=[
            pltpu.VMEM((4, nclip, width), F32),
            pltpu.VMEM((4, ndose, width), F32),
            pltpu.VMEM((4, nfocus, width), F32),
        ]
        + [pltpu.VMEM(ids[0].shape, jnp.int32)] * 3
        + [
            pltpu.VMEM((512, 256), F32),
            pltpu.VMEM((512, 256), F32),
            pltpu.VMEM((nclip, cols), BF16),
            pltpu.VMEM((nclip, cols), BF16),
            pltpu.VMEM((cols, nclip), F32),
            pltpu.VMEM((ndose, cols), F32),
            pltpu.VMEM((cols, 128), F32),
            pltpu.VMEM((cols, cols), F32),
            pltpu.VMEM((cols, cols), F32),
            pltpu.SemaphoreType.DMA((18,)),
            pltpu.SemaphoreType.DMA((18,)),
            pltpu.SemaphoreType.DMA((6,)),
        ],
        compiler_params=pltpu.CompilerParams(
            collective_id=0, has_side_effects=True, vmem_limit_bytes=48 * 2**20
        ),
        name="exchange",
    )(clip_cache, dose_scale, focus_term, *ids)


def compute(
    total, ch_in, cl_in, ds_in, fs_in, gram_in, clips, doses, focuses, out,
    ch, cl, ds, fs, gram, place, where, sem, dcol, table, wd, state, rows, out_sem,
):
    pairs = (gram_in, gram), (fs_in, fs), (ds_in, ds), (ch_in, ch), (cl_in, cl)
    copies = [pltpu.make_async_copy(source, target, sem.at[n]) for n, (source, target) in enumerate(pairs)]
    for copy in copies:
        copy.start()
    nclip, cols = ch.shape
    ndose, nfocus = ds.shape[1], fs.shape[1]
    place[...] = doses[...] * nclip + clips[...]
    copies.append(pltpu.make_async_copy(place, where, sem.at[5]))
    copies[5].start()
    for copy in copies[:3]:
        copy.wait()
    fall = jnp.concatenate([fs[p] for p in range(4)], axis=1)
    for p in range(4):
        dcol[p * 128 : (p + 1) * 128, :] = jnp.concatenate([ds[p], jnp.zeros((128 - ndose, 128), F32)], axis=0).T

    row_i = lax.broadcasted_iota(jnp.int32, (128, 128), 0)
    col_i = lax.broadcasted_iota(jnp.int32, (128, 128), 1)
    squares = jnp.concatenate(
        [
            jnp.sum(jnp.where(row_i == col_i, gram[p * 128 : (p + 1) * 128, p * 128 : (p + 1) * 128], 0.0), axis=0, keepdims=True)
            for p in range(4)
        ],
        axis=1,
    )
    inverse_norm = 1.0 / jnp.sqrt(squares / total + EPSILON)
    norm_col = column(inverse_norm)
    d = squares * inverse_norm * inverse_norm
    d_col = column(d)
    g_prev = gram[:256, :256] * norm_col[:256] * inverse_norm[:, :256]
    g_cross = gram[:256, 256:] * norm_col[:256] * inverse_norm[:, 256:]
    g_own = gram[256:, 256:] * norm_col[256:] * inverse_norm[:, 256:]
    b_prev = 0.5 * g_prev[:128, 128:] / (d_col[:128] + d[:, 128:256])
    b_own = 0.5 * g_own[:128, 128:] / (d_col[256:384] + d[:, 384:])
    (m_prev, m_own), eye = inverses([b_prev, b_own], state)
    z = 2.0 * full(m_prev, b_prev)
    q_right = jnp.concatenate([z, eye - full(b_prev, z, TN)], axis=0)
    q_left = jnp.concatenate([2.0 * m_own - eye, -2.0 * full(b_own, m_own, TN)], axis=0)

    cross = full(full(q_right, g_cross, TN), q_left)
    d_left = jnp.sum(q_right * full(g_prev, q_right), axis=0, keepdims=True)
    d_right = jnp.sum(q_left * full(g_own, q_left), axis=0, keepdims=True)
    b = 0.5 * cross / (column(d_left) + d_right)
    (m,), _ = inverses([b], state)
    z = 2.0 * full(m, b)
    odd = lax.axis_index("panel") % 2 == 1
    top = jnp.where(odd, z, 2.0 * m - eye)
    bottom = jnp.where(odd, eye - full(b, z, TN), -2.0 * full(b, m, TN))
    w = jnp.concatenate([full(q_right, top), full(q_left, bottom)], axis=0) * norm_col
    wd[...] = w

    parts = jnp.concatenate(three(full(fall, w)), axis=0)
    setting = lax.broadcasted_iota(jnp.int32, (3 * nfocus, 128), 0) % nfocus

    def focus(step, _):
        for u in range(8):
            r = step * 8 + u
            chosen = jnp.where(setting == focuses[pl.ds(r, 1), :], 1.0, 0.0).astype(BF16)
            rows[pl.ds(pl.multiple_of(r * 128, 128), 128), :] = dot(chosen, parts, TN)
        return 0

    lax.fori_loop(0, focuses.shape[0] // 8, focus, 0)

    for copy in copies[3:]:
        copy.wait()
    lane = lax.broadcasted_iota(jnp.int32, (cols, 128), 1)

    def rows_of(pair, _):
        scaled = []
        for e in range(2):
            dj = jnp.sum(jnp.where(lane == pair * 2 + e, dcol[...], 0.0), axis=1, keepdims=True)
            scaled.append(wd[...] * dj)
        wh, wl = split(jnp.concatenate(scaled, axis=1))
        for m in range(nclip // 256):
            here = pl.ds(m * 256, 256)
            part = dot(ch[here, :], wh) + dot(cl[here, :], wh) + dot(ch[here, :], wl)
            for e in range(2):
                begin = pl.multiple_of((pair * 2 + e) * nclip + m * 256, 256)
                table[pl.ds(begin, 256), :] = part[:, e * 128 : (e + 1) * 128]
        return 0

    lax.fori_loop(0, ndose // 2, rows_of, 0)

    chunks = out_sem.shape[0]
    height = rows.shape[0] // chunks

    def written(chunk):
        here = pl.ds(pl.multiple_of(chunk * height, height), height)
        return pltpu.make_async_copy(rows.at[here, :], out.at[here, :], out_sem.at[chunk])

    def gather(line, _):
        for u in range(128 // 8):
            begin = pl.multiple_of(line * 128 + u * 8, 8)
            found = jnp.concatenate([table[pl.ds(where[line, u * 8 + e], 1), :] for e in range(8)], axis=0)
            rows[pl.ds(begin, 8), :] = rows[pl.ds(begin, 8), :] + found
        return 0

    for chunk in range(chunks):
        lines = height // 128
        lax.fori_loop(chunk * lines, (chunk + 1) * lines, gather, 0)
        written(chunk).start()
    for chunk in range(chunks):
        written(chunk).wait()


def call_compute(total, ch, cl, ds, fs, gram, ids):
    lines = ids[0].shape[0]
    nclip, cols = ch.shape
    _, ndose, width = ds.shape
    operands = (ch, cl, ds, fs, gram)
    return pl.pallas_call(
        functools.partial(compute, float(total)),
        out_shape=jax.ShapeDtypeStruct((lines * 128, width), F32),
        in_specs=[ANY] * 5 + [VMEM] * 3,
        out_specs=ANY,
        scratch_shapes=[pltpu.VMEM(a.shape, a.dtype) for a in operands]
        + [
            pltpu.VMEM((lines, 128), jnp.int32),
            pltpu.SMEM((lines, 128), jnp.int32),
            pltpu.SemaphoreType.DMA((6,)),
            pltpu.VMEM((cols, 128), F32),
            pltpu.VMEM((ndose * nclip, width), F32),
            pltpu.VMEM((cols, width), F32),
            pltpu.VMEM((2, 2 * width, width), F32),
            pltpu.VMEM((lines * 128, width), F32),
            pltpu.SemaphoreType.DMA((8,)),
        ],
        compiler_params=pltpu.CompilerParams(vmem_limit_bytes=48 * 2**20),
        name="compute",
    )(*operands, *ids)


def shards(clip_cache, dose_scale, focus_term, clip_ids, dose_ids, focus_ids):
    rows = clip_ids.shape[0]
    ids = [a.reshape(rows // 128, 128) for a in (clip_ids, dose_ids, focus_ids)]
    gathered = call_exchange(lax.axis_size("panel"), clip_cache, dose_scale, focus_term, ids)
    return call_compute(rows * lax.axis_size("slab"), *gathered, ids)


def solution(mesh):
    return jax.shard_map(
        shards,
        mesh=mesh,
        in_specs=(
            P(None, "panel"),
            P(None, "panel"),
            P(None, "panel"),
            P("slab"),
            P("slab"),
            P("slab"),
        ),
        out_specs=P("slab", "panel"),
        check_vma=False,
    )
```

```python
import functools

import jax
import jax.numpy as jnp
from jax import lax
from jax.experimental import pallas as pl
from jax.experimental.pallas import tpu as pltpu
from jax.sharding import PartitionSpec as P

MESH = pl.DeviceIdType.MESH
EPSILON = 1e-06
F32 = jnp.float32
BF16 = jnp.bfloat16
ANY = pl.BlockSpec(memory_space=pl.ANY)


def split(value):
    high = value.astype(BF16)
    return high, (value - high.astype(F32)).astype(BF16)


def dot(a, b, dims=((1,), (0,))):
    return lax.dot_general(a, b, (dims, ((), ())), preferred_element_type=F32)


def three(value):
    high = value.astype(BF16)
    rest = value - high.astype(F32)
    middle = rest.astype(BF16)
    return high, middle, (rest - middle.astype(F32)).astype(BF16)


def full(a, b, dims=((1,), (0,))):
    a1, a2, a3 = three(a)
    b1, b2, b3 = three(b)
    small = dot(a2, b2, dims) + dot(a1, b3, dims) + dot(a3, b1, dims)
    return dot(a1, b1, dims) + (dot(a1, b2, dims) + dot(a2, b1, dims) + small)


TN = ((0,), (0,))
NT = ((1,), (1,))


def column(row):
    return jnp.broadcast_to(row, (128, row.shape[1])).T[:, :1]


def inverses(bs, state):
    n = bs[0].shape[0]
    eye = (lax.broadcasted_iota(jnp.int32, (n, n), 0) == lax.broadcasted_iota(jnp.int32, (n, n), 1)).astype(F32)
    squares = [full(b, b, NT) for b in bs]
    bound = functools.reduce(jnp.maximum, [jnp.max(jnp.sum(jnp.abs(s), axis=1)) for s in squares])
    scale = 2.0 / (2.0 + bound)
    for e, s in enumerate(squares):
        rest = (1.0 - scale) * eye - scale * s
        state[e, :n, :] = scale * (eye + rest)
        state[e, n:, :] = full(rest, rest)
    ratio = bound / (2.0 + bound)

    def body(ratio):
        for e in range(len(bs)):
            old = state[e]
            new = full(old, old[n:])
            state[e, :n, :] = old[:n] + new[:n]
            state[e, n:, :] = new[n:]
        return ratio * ratio

    lax.while_loop(lambda ratio: ratio > 1e-8, body, ratio * ratio)
    return [state[e, :n, :] for e in range(len(bs))], eye


def onehot(places, count, offset):
    value = jnp.broadcast_to(places.astype(F32) - offset, (16, places.shape[1])).astype(BF16)
    tile = lax.broadcasted_iota(jnp.int32, (16, places.shape[1]), 0).astype(F32)
    one, none = jnp.ones_like(value), jnp.zeros_like(value)
    return [jnp.where((tile + 16.0 * t).astype(BF16) == value, one, none) for t in range(count // 16)]


def count_ids(counts, clips, doses, focuses):
    rows = 8

    def count(step, _):
        here = pl.ds(pl.multiple_of(step * rows, rows), rows)
        clip = clips[here, :]
        first = (clip // 256) * 128 + doses[here, :] * 8 + focuses[here, :]
        second = clip % 256
        tall, wide = [], []
        for r in range(rows):
            row = first[r : r + 1, :]
            tall.append(jnp.concatenate(onehot(row, 256, 0.0) + onehot(row, 256, 256.0), axis=0))
            wide.append(jnp.concatenate(onehot(second[r : r + 1, :], 256, 0.0), axis=0))
        counts[...] += dot(jnp.concatenate(tall, axis=1), jnp.concatenate(wide, axis=1), NT)
        return 0

    lax.fori_loop(0, clips.shape[0] // rows, count, 0)


def exchange(
    seats, c_ref, d_ref, f_ref, i_ref, j_ref, k_ref, ch_out, cl_out, ds_out, fs_out, gram_out,
    cs, ds, fs, ci, di, fi, oi, oj, ok, counts, counts_twin, ch, cl, ct, frow, srow, drow, dcol, gram, gram_twin, send_sem, recv_sem, local_sem, out_sem,
):
    seat = lax.axis_index("panel")
    slab = lax.axis_index("slab")
    z_hi, core = slab // 2, slab % 2
    side = seat % 2
    base = seat - side
    nclip, width = c_ref.shape
    ndose, nfocus = d_ref.shape[0], f_ref.shape[0]
    cols = 4 * width
    half = nclip // 2

    def near(target):
        z_lo = target % 4
        other = jnp.where((z_lo == 0) | (z_lo == 3), 1, 0)
        return (z_hi + other) % 2

    partner = (seat + 1 - 2 * side, slab)
    next0 = (base + 2) % seats
    next1 = (base + 3) % seats
    to_next0 = (next0, near(next0) * 2 + core)
    to_next1 = (next1, near(next1) * 2 + core)
    from_group = near(seat) * 2 + core
    from_prev0 = ((base + seats - 2) % seats, from_group)
    from_prev1 = ((base + seats - 1) % seats, from_group)
    z_lo = seat % 4
    mirror = (seat - z_lo + 3 - z_lo, (1 - z_hi) * 2 + core)
    twin = (seat, z_hi * 2 + 1 - core)

    own = 2 + side
    pairs = (i_ref, oi), (j_ref, oj), (k_ref, ok), (c_ref, cs.at[own]), (d_ref, ds.at[own]), (f_ref, fs.at[own])
    local = [pltpu.make_async_copy(source, target, local_sem.at[n]) for n, (source, target) in enumerate(pairs)]
    for copy in local:
        copy.start()
    barrier = pltpu.get_barrier_semaphore()
    for device in (partner, from_prev0, from_prev1, mirror, twin):
        pl.semaphore_signal(barrier, inc=1, device_id=device, device_id_type=MESH)
    pl.semaphore_wait(barrier, 5)

    def remote(number, source, target, device, arrival=None):
        return pltpu.make_async_remote_copy(
            src_ref=source,
            dst_ref=target,
            send_sem=send_sem.at[number],
            recv_sem=recv_sem.at[number if arrival is None else arrival],
            device_id=device,
            device_id_type=MESH,
        )

    mine = pl.ds(pl.multiple_of(core * half, 128), half)
    mate = 3 - side
    ids = (i_ref, ci), (j_ref, di), (k_ref, fi)

    sent = []
    for n, (source, target) in enumerate(ids):
        sent.append(remote(n, source, target, mirror))
    sent.append(remote(3, c_ref.at[mine], cs.at[own, mine], partner))
    sent.append(remote(6, d_ref, ds.at[own], partner))
    sent.append(remote(9, f_ref, fs.at[own], partner))
    for n, device in enumerate((to_next0, to_next1)):
        sent.append(remote(4 + n, c_ref.at[mine], cs.at[side, mine], device, 4 + side))
        sent.append(remote(7 + n, d_ref, ds.at[side], device, 7 + side))
        sent.append(remote(10 + n, f_ref, fs.at[side], device, 10 + side))
    for copy in sent:
        copy.start()

    counts[...] = jnp.zeros_like(counts)
    for copy in local:
        copy.wait()
    count_ids(counts, oi, oj, ok)
    for n, (source, target) in enumerate(ids):
        remote(n, source, target, mirror).wait_recv()
    count_ids(counts, ci, di, fi)
    mine_counts = pl.ds(pl.multiple_of(core * 256, 256), 256)
    theirs_counts = pl.ds(pl.multiple_of((1 - core) * 256, 256), 256)
    swap_counts = remote(15, counts.at[theirs_counts], counts_twin, twin)
    swap_counts.start()

    def arrived(n, slot):
        remote(n, c_ref.at[mine], cs.at[slot, mine], partner).wait_recv()
        remote(n + 3, d_ref, ds.at[slot], partner).wait_recv()
        remote(n + 6, f_ref, fs.at[slot], partner).wait_recv()
        forward = remote(9 + n, cs.at[slot, mine], cs.at[slot, mine], twin)
        forward.start()
        sent.append(forward)

    def halve(p, rows):
        high, low = split(cs[p, rows, :])
        ch[rows, p * width : (p + 1) * width] = high
        cl[rows, p * width : (p + 1) * width] = low

    def prepare(m):
        for p in (2 * m, 2 * m + 1):
            halve(p, mine)
            lanes = pl.ds(p * width, width)
            ct[lanes, :] = cs[p, mine, :].T
            frow[:, lanes] = fs[p]
            drow[:, lanes] = ds[p]
            dcol[lanes, :] = jnp.concatenate([ds[p], jnp.zeros((128 - ndose, width), F32)], axis=0).T

    def focus_terms(m):
        here = pl.ds(m * 256, 256)
        n = jnp.concatenate([counts[pl.ds(pl.multiple_of(core * 256 + h * 128, 128), 128), :] for h in range(2)], axis=1)
        nh, nl = split(n)
        v = dot(nh, ch[mine, here]) + dot(nh, cl[mine, here]) + dot(nl, ch[mine, here])
        s = jnp.zeros((nfocus, 256), F32)
        per_focus = jnp.zeros((nfocus, half), F32)
        for j in range(ndose):
            s = s + v[j * nfocus : (j + 1) * nfocus, :] * drow[j : j + 1, here]
            per_focus = per_focus + n[j * nfocus : (j + 1) * nfocus, :]
        srow[:, here] = s + 0.5 * jnp.sum(per_focus, axis=1, keepdims=True) * frow[:, here]
        right = pl.ds(m * 256, cols - m * 256)
        left = jnp.concatenate([srow[:, here], frow[:, here]], axis=0)
        gram[here, right] = full(left, jnp.concatenate([frow[:, right], srow[:, right]], axis=0), TN)

    lane = lax.broadcasted_iota(jnp.int32, (256, 128), 1)
    unroll = 4

    def table_terms(m):
        here = pl.ds(m * 256, 256)

        def dose(step, _):
            left = []
            for e in range(unroll):
                j = step * unroll + e
                at = pl.multiple_of(core * 256 + j * nfocus, nfocus)
                nj = jnp.concatenate(
                    [jnp.sum(counts[pl.ds(at + h * 128, nfocus), :], axis=0, keepdims=True) for h in range(2)], axis=1
                )
                dj = jnp.sum(jnp.where(lane == j, dcol[here, :], 0.0), axis=1, keepdims=True)
                left.append(split(ct[here, :] * nj * dj))
            for r in range(m, 2):
                right = pl.ds(r * 256, 256)
                total = gram[here, right]
                for e, (uh, ul) in enumerate(left):
                    part = dot(uh, ch[mine, right]) + dot(uh, cl[mine, right]) + dot(ul, ch[mine, right])
                    total = total + part * drow[pl.ds(step * unroll + e, 1), right]
                gram[here, right] = total
            return 0

        lax.fori_loop(0, ndose // unroll, dose, 0)
        right = pl.ds(m * 256, cols - m * 256)
        swap = remote(16 + m, gram.at[here, right], gram_twin.at[here, right], twin)
        swap.start()
        return swap

    arrived(3, mate)
    prepare(1)
    swap_counts.wait()
    counts[mine_counts, :] += counts_twin[...]
    focus_terms(1)
    swaps = [(1, table_terms(1))]
    arrived(4, 0)
    arrived(5, 1)
    prepare(0)
    focus_terms(0)
    swaps.append((0, table_terms(0)))

    theirs = pl.ds(pl.multiple_of((1 - core) * half, 128), half)
    for n, slot in ((12, mate), (13, 0), (14, 1)):
        remote(n, c_ref.at[theirs], cs.at[slot, theirs], twin).wait_recv()
    for p in range(4):
        halve(p, theirs)
    outs = [
        pltpu.make_async_copy(source, target, out_sem.at[n])
        for n, (source, target) in enumerate(((ch, ch_out), (cl, cl_out), (ds, ds_out), (fs, fs_out)))
    ]
    for out in outs:
        out.start()
    for m, swap in swaps:
        swap.wait()
        here = pl.ds(m * 256, 256)
        right = pl.ds(m * 256, cols - m * 256)
        gram[here, right] += gram_twin[here, right]
        out = pltpu.make_async_copy(gram.at[here, right], gram_out.at[here, right], out_sem.at[4 + m])
        out.start()
        outs.append(out)
    for copy in sent:
        copy.wait_send()
    for out in outs:
        out.wait()


def call_exchange(seats, clip_cache, dose_scale, focus_term, ids):
    nclip, width = clip_cache.shape
    ndose, nfocus = dose_scale.shape[0], focus_term.shape[0]
    cols = 4 * width
    out = [((nclip, cols), BF16)] * 2 + [((4, ndose, width), F32), ((4, nfocus, width), F32), ((cols, cols), F32)]
    return pl.pallas_call(
        functools.partial(exchange, seats),
        out_shape=[jax.ShapeDtypeStruct(*o) for o in out],
        in_specs=[ANY] * 6,
        out_specs=[ANY] * 5,
        scratch_shapes=[
            pltpu.VMEM((4, nclip, width), F32),
            pltpu.VMEM((4, ndose, width), F32),
            pltpu.VMEM((4, nfocus, width), F32),
        ]
        + [pltpu.VMEM(ids[0].shape, jnp.int32)] * 6
        + [
            pltpu.VMEM((512, 256), F32),
            pltpu.VMEM((256, 256), F32),
            pltpu.VMEM((nclip, cols), BF16),
            pltpu.VMEM((nclip, cols), BF16),
            pltpu.VMEM((cols, nclip // 2), F32),
            pltpu.VMEM((nfocus, cols), F32),
            pltpu.VMEM((nfocus, cols), F32),
            pltpu.VMEM((ndose, cols), F32),
            pltpu.VMEM((cols, 128), F32),
            pltpu.VMEM((cols, cols), F32),
            pltpu.VMEM((cols, cols), F32),
            pltpu.SemaphoreType.DMA((18,)),
            pltpu.SemaphoreType.DMA((18,)),
            pltpu.SemaphoreType.DMA((6,)),
            pltpu.SemaphoreType.DMA((6,)),
        ],
        compiler_params=pltpu.CompilerParams(
            collective_id=0, has_side_effects=True, vmem_limit_bytes=56 * 2**20
        ),
        name="exchange",
    )(clip_cache, dose_scale, focus_term, *ids)


def compute(
    total, ch_in, cl_in, ds_in, fs_in, gram_in, clips_in, doses_in, focuses_in, out,
    ch, cl, ds, fs, gram, clips, doses, focuses, place, where, sem, dcol, table, wd, state, rows, out_sem,
):
    pairs = (clips_in, clips), (doses_in, doses), (focuses_in, focuses), (gram_in, gram), (fs_in, fs), (ds_in, ds)
    pairs += (ch_in, ch), (cl_in, cl)
    copies = [pltpu.make_async_copy(source, target, sem.at[n]) for n, (source, target) in enumerate(pairs)]
    for copy in copies:
        copy.start()
    nclip, cols = ch.shape
    ndose, nfocus = ds.shape[1], fs.shape[1]
    for copy in copies[:3]:
        copy.wait()
    place[...] = doses[...] * nclip + clips[...]
    copies.append(pltpu.make_async_copy(place, where, sem.at[8]))
    copies[8].start()
    for copy in copies[3:6]:
        copy.wait()
    fall = jnp.concatenate([fs[p] for p in range(4)], axis=1)
    for p in range(4):
        dcol[p * 128 : (p + 1) * 128, :] = jnp.concatenate([ds[p], jnp.zeros((128 - ndose, 128), F32)], axis=0).T

    row_i = lax.broadcasted_iota(jnp.int32, (128, 128), 0)
    col_i = lax.broadcasted_iota(jnp.int32, (128, 128), 1)
    squares = jnp.concatenate(
        [
            jnp.sum(jnp.where(row_i == col_i, gram[p * 128 : (p + 1) * 128, p * 128 : (p + 1) * 128], 0.0), axis=0, keepdims=True)
            for p in range(4)
        ],
        axis=1,
    )
    inverse_norm = 1.0 / jnp.sqrt(squares / total + EPSILON)
    norm_col = column(inverse_norm)
    d = squares * inverse_norm * inverse_norm
    d_col = column(d)
    g_prev = gram[:256, :256] * norm_col[:256] * inverse_norm[:, :256]
    g_cross = gram[:256, 256:] * norm_col[:256] * inverse_norm[:, 256:]
    g_own = gram[256:, 256:] * norm_col[256:] * inverse_norm[:, 256:]
    b_prev = 0.5 * g_prev[:128, 128:] / (d_col[:128] + d[:, 128:256])
    b_own = 0.5 * g_own[:128, 128:] / (d_col[256:384] + d[:, 384:])
    (m_prev, m_own), eye = inverses([b_prev, b_own], state)
    z = 2.0 * full(m_prev, b_prev)
    q_right = jnp.concatenate([z, eye - full(b_prev, z, TN)], axis=0)
    q_left = jnp.concatenate([2.0 * m_own - eye, -2.0 * full(b_own, m_own, TN)], axis=0)

    cross = full(full(q_right, g_cross, TN), q_left)
    d_left = jnp.sum(q_right * full(g_prev, q_right), axis=0, keepdims=True)
    d_right = jnp.sum(q_left * full(g_own, q_left), axis=0, keepdims=True)
    b = 0.5 * cross / (column(d_left) + d_right)
    (m,), _ = inverses([b], state)
    z = 2.0 * full(m, b)
    odd = lax.axis_index("panel") % 2 == 1
    top = jnp.where(odd, z, 2.0 * m - eye)
    bottom = jnp.where(odd, eye - full(b, z, TN), -2.0 * full(b, m, TN))
    w = jnp.concatenate([full(q_right, top), full(q_left, bottom)], axis=0) * norm_col
    wd[...] = w

    parts = jnp.concatenate(three(full(fall, w)), axis=0)
    setting = lax.broadcasted_iota(jnp.int32, (3 * nfocus, 128), 0) % nfocus

    def focus(step, _):
        for u in range(8):
            r = step * 8 + u
            chosen = jnp.where(setting == focuses[pl.ds(r, 1), :], 1.0, 0.0).astype(BF16)
            rows[pl.ds(pl.multiple_of(r * 128, 128), 128), :] = dot(chosen, parts, TN)
        return 0

    lax.fori_loop(0, focuses.shape[0] // 8, focus, 0)

    for copy in copies[6:]:
        copy.wait()
    lane = lax.broadcasted_iota(jnp.int32, (cols, 128), 1)

    def rows_of(pair, _):
        scaled = []
        for e in range(2):
            dj = jnp.sum(jnp.where(lane == pair * 2 + e, dcol[...], 0.0), axis=1, keepdims=True)
            scaled.append(wd[...] * dj)
        wh, wl = split(jnp.concatenate(scaled, axis=1))
        for m in range(nclip // 256):
            here = pl.ds(m * 256, 256)
            part = dot(ch[here, :], wh) + dot(cl[here, :], wh) + dot(ch[here, :], wl)
            for e in range(2):
                begin = pl.multiple_of((pair * 2 + e) * nclip + m * 256, 256)
                table[pl.ds(begin, 256), :] = part[:, e * 128 : (e + 1) * 128]
        return 0

    lax.fori_loop(0, ndose // 4, lambda q, c: rows_of(q * 2 + 1, rows_of(q * 2, c)), 0)

    chunks = out_sem.shape[0]
    height = rows.shape[0] // chunks

    def written(chunk):
        here = pl.ds(pl.multiple_of(chunk * height, height), height)
        return pltpu.make_async_copy(rows.at[here, :], out.at[here, :], out_sem.at[chunk])

    def gather(line, _):
        for u in range(128 // 8):
            begin = pl.multiple_of(line * 128 + u * 8, 8)
            found = jnp.concatenate([table[pl.ds(where[line, u * 8 + e], 1), :] for e in range(8)], axis=0)
            rows[pl.ds(begin, 8), :] = rows[pl.ds(begin, 8), :] + found
        return 0

    for chunk in range(chunks):
        lines = height // 128
        lax.fori_loop(chunk * lines, (chunk + 1) * lines, gather, 0)
        written(chunk).start()
    for chunk in range(chunks):
        written(chunk).wait()


def call_compute(total, ch, cl, ds, fs, gram, ids):
    lines = ids[0].shape[0]
    nclip, cols = ch.shape
    _, ndose, width = ds.shape
    operands = (ch, cl, ds, fs, gram, *ids)
    return pl.pallas_call(
        functools.partial(compute, float(total)),
        out_shape=jax.ShapeDtypeStruct((lines * 128, width), F32),
        in_specs=[ANY] * 8,
        out_specs=ANY,
        scratch_shapes=[pltpu.VMEM(a.shape, a.dtype) for a in operands]
        + [
            pltpu.VMEM((lines, 128), jnp.int32),
            pltpu.SMEM((lines, 128), jnp.int32),
            pltpu.SemaphoreType.DMA((9,)),
            pltpu.VMEM((cols, 128), F32),
            pltpu.VMEM((ndose * nclip, width), F32),
            pltpu.VMEM((cols, width), F32),
            pltpu.VMEM((2, 2 * width, width), F32),
            pltpu.VMEM((lines * 128, width), F32),
            pltpu.SemaphoreType.DMA((8,)),
        ],
        compiler_params=pltpu.CompilerParams(vmem_limit_bytes=56 * 2**20),
        name="compute",
    )(*operands)


def shards(clip_cache, dose_scale, focus_term, clip_ids, dose_ids, focus_ids):
    rows = clip_ids.shape[0]
    ids = [a.reshape(rows // 128, 128) for a in (clip_ids, dose_ids, focus_ids)]
    gathered = call_exchange(lax.axis_size("panel"), clip_cache, dose_scale, focus_term, ids)
    return call_compute(rows * lax.axis_size("slab"), *gathered, ids)


def solution(mesh):
    return jax.shard_map(
        shards,
        mesh=mesh,
        in_specs=(
            P(None, "panel"),
            P(None, "panel"),
            P(None, "panel"),
            P("slab"),
            P("slab"),
            P("slab"),
        ),
        out_specs=P("slab", "panel"),
        check_vma=False,
    )
```

```python
import functools

import jax
import jax.numpy as jnp
from jax import lax
from jax.experimental import pallas as pl
from jax.experimental.pallas import tpu as pltpu
from jax.sharding import PartitionSpec as P

MESH = pl.DeviceIdType.MESH
EPSILON = 1e-06
F32 = jnp.float32
BF16 = jnp.bfloat16
ANY = pl.BlockSpec(memory_space=pl.ANY)


def split(value):
    high = value.astype(BF16)
    return high, (value - high.astype(F32)).astype(BF16)


def dot(a, b, dims=((1,), (0,))):
    return lax.dot_general(a, b, (dims, ((), ())), preferred_element_type=F32)


def three(value):
    high = value.astype(BF16)
    rest = value - high.astype(F32)
    middle = rest.astype(BF16)
    return high, middle, (rest - middle.astype(F32)).astype(BF16)


def full(a, b, dims=((1,), (0,))):
    a1, a2, a3 = three(a)
    b1, b2, b3 = three(b)
    small = dot(a2, b2, dims) + dot(a1, b3, dims) + dot(a3, b1, dims)
    return dot(a1, b1, dims) + (dot(a1, b2, dims) + dot(a2, b1, dims) + small)


def good(a, b, dims=((1,), (0,))):
    a1, a2 = split(a)
    b1, b2 = split(b)
    return dot(a1, b1, dims) + (dot(a1, b2, dims) + dot(a2, b1, dims))


TN = ((0,), (0,))
NT = ((1,), (1,))


def column(row):
    return jnp.broadcast_to(row, (128, row.shape[1])).T[:, :1]


def inverses(bs, state):
    n = bs[0].shape[0]
    eye = (lax.broadcasted_iota(jnp.int32, (n, n), 0) == lax.broadcasted_iota(jnp.int32, (n, n), 1)).astype(F32)
    squares = [full(b, b, NT) for b in bs]
    bound = functools.reduce(jnp.maximum, [jnp.max(jnp.sum(jnp.abs(s), axis=1)) for s in squares])
    scale = 2.0 / (2.0 + bound)
    for e, s in enumerate(squares):
        rest = (1.0 - scale) * eye - scale * s
        state[e, :n, :] = scale * (eye + rest)
        state[e, n:, :] = full(rest, rest)
    ratio = bound / (2.0 + bound)

    def body(ratio):
        for e in range(len(bs)):
            old = state[e]
            new = full(old, old[n:])
            state[e, :n, :] = old[:n] + new[:n]
            state[e, n:, :] = new[n:]
        return ratio * ratio

    lax.while_loop(lambda ratio: ratio > 1e-8, body, ratio * ratio)
    return [state[e, :n, :] for e in range(len(bs))], eye


def onehot(places, count, offset):
    value = jnp.broadcast_to(places.astype(F32) - offset, (16, places.shape[1])).astype(BF16)
    tile = lax.broadcasted_iota(jnp.int32, (16, places.shape[1]), 0).astype(F32)
    one, none = jnp.ones_like(value), jnp.zeros_like(value)
    return [jnp.where((tile + 16.0 * t).astype(BF16) == value, one, none) for t in range(count // 16)]


def count_ids(counts, clips, doses, focuses):
    rows = 8

    def count(step, _):
        here = pl.ds(pl.multiple_of(step * rows, rows), rows)
        clip = clips[here, :]
        first = (clip // 256) * 128 + doses[here, :] * 8 + focuses[here, :]
        second = clip % 256
        tall, wide = [], []
        for r in range(rows):
            row = first[r : r + 1, :]
            tall.append(jnp.concatenate(onehot(row, 256, 0.0) + onehot(row, 256, 256.0), axis=0))
            wide.append(jnp.concatenate(onehot(second[r : r + 1, :], 256, 0.0), axis=0))
        counts[...] += dot(jnp.concatenate(tall, axis=1), jnp.concatenate(wide, axis=1), NT)
        return 0

    lax.fori_loop(0, clips.shape[0] // rows, count, 0)


def exchange(
    seats, c_ref, d_ref, f_ref, i_ref, j_ref, k_ref, ch_out, cl_out, ds_out, fs_out, gram_out,
    cs, ds, fs, ci, di, fi, oi, oj, ok, counts, counts_twin, ch, cl, ct, frow, srow, drow, dcol, gram, gram_twin, send_sem, recv_sem, local_sem, out_sem,
):
    seat = lax.axis_index("panel")
    slab = lax.axis_index("slab")
    z_hi, core = slab // 2, slab % 2
    side = seat % 2
    base = seat - side
    nclip, width = c_ref.shape
    ndose, nfocus = d_ref.shape[0], f_ref.shape[0]
    cols = 4 * width
    half = nclip // 2

    def near(target):
        z_lo = target % 4
        other = jnp.where((z_lo == 0) | (z_lo == 3), 1, 0)
        return (z_hi + other) % 2

    partner = (seat + 1 - 2 * side, slab)
    next0 = (base + 2) % seats
    next1 = (base + 3) % seats
    to_next0 = (next0, near(next0) * 2 + core)
    to_next1 = (next1, near(next1) * 2 + core)
    from_group = near(seat) * 2 + core
    from_prev0 = ((base + seats - 2) % seats, from_group)
    from_prev1 = ((base + seats - 1) % seats, from_group)
    z_lo = seat % 4
    mirror = (seat - z_lo + 3 - z_lo, (1 - z_hi) * 2 + core)
    twin = (seat, z_hi * 2 + 1 - core)

    own = 2 + side
    pairs = (i_ref, oi), (j_ref, oj), (k_ref, ok), (c_ref, cs.at[own]), (d_ref, ds.at[own]), (f_ref, fs.at[own])
    local = [pltpu.make_async_copy(source, target, local_sem.at[n]) for n, (source, target) in enumerate(pairs)]
    for copy in local:
        copy.start()
    barrier = pltpu.get_barrier_semaphore()
    for device in (partner, from_prev0, from_prev1, mirror, twin):
        pl.semaphore_signal(barrier, inc=1, device_id=device, device_id_type=MESH)
    pl.semaphore_wait(barrier, 5)

    def remote(number, source, target, device, arrival=None):
        return pltpu.make_async_remote_copy(
            src_ref=source,
            dst_ref=target,
            send_sem=send_sem.at[number],
            recv_sem=recv_sem.at[number if arrival is None else arrival],
            device_id=device,
            device_id_type=MESH,
        )

    mine = pl.ds(pl.multiple_of(core * half, 128), half)
    mate = 3 - side
    ids = (i_ref, ci), (j_ref, di), (k_ref, fi)

    sent = []
    for n, (source, target) in enumerate(ids):
        sent.append(remote(n, source, target, mirror))
    sent.append(remote(3, c_ref.at[mine], cs.at[own, mine], partner))
    sent.append(remote(6, d_ref, ds.at[own], partner))
    sent.append(remote(9, f_ref, fs.at[own], partner))
    for n, device in enumerate((to_next0, to_next1)):
        sent.append(remote(4 + n, c_ref.at[mine], cs.at[side, mine], device, 4 + side))
        sent.append(remote(7 + n, d_ref, ds.at[side], device, 7 + side))
        sent.append(remote(10 + n, f_ref, fs.at[side], device, 10 + side))
    for copy in sent:
        copy.start()

    counts[...] = jnp.zeros_like(counts)
    for copy in local:
        copy.wait()
    count_ids(counts, oi, oj, ok)
    for n, (source, target) in enumerate(ids):
        remote(n, source, target, mirror).wait_recv()
    count_ids(counts, ci, di, fi)
    mine_counts = pl.ds(pl.multiple_of(core * 256, 256), 256)
    theirs_counts = pl.ds(pl.multiple_of((1 - core) * 256, 256), 256)
    swap_counts = remote(15, counts.at[theirs_counts], counts_twin, twin)
    swap_counts.start()

    def arrived(n, slot):
        remote(n, c_ref.at[mine], cs.at[slot, mine], partner).wait_recv()
        remote(n + 3, d_ref, ds.at[slot], partner).wait_recv()
        remote(n + 6, f_ref, fs.at[slot], partner).wait_recv()
        forward = remote(9 + n, cs.at[slot, mine], cs.at[slot, mine], twin)
        forward.start()
        sent.append(forward)

    def halve(p, rows):
        high, low = split(cs[p, rows, :])
        ch[rows, p * width : (p + 1) * width] = high
        cl[rows, p * width : (p + 1) * width] = low

    def prepare(m):
        for p in (2 * m, 2 * m + 1):
            halve(p, mine)
            lanes = pl.ds(p * width, width)
            ct[lanes, :] = cs[p, mine, :].T
            frow[:, lanes] = fs[p]
            drow[:, lanes] = ds[p]
            dcol[lanes, :] = jnp.concatenate([ds[p], jnp.zeros((128 - ndose, width), F32)], axis=0).T

    def focus_terms(m):
        here = pl.ds(m * 256, 256)
        n = jnp.concatenate([counts[pl.ds(pl.multiple_of(core * 256 + h * 128, 128), 128), :] for h in range(2)], axis=1)
        nh, nl = split(n)
        v = dot(nh, ch[mine, here]) + dot(nh, cl[mine, here]) + dot(nl, ch[mine, here])
        s = jnp.zeros((nfocus, 256), F32)
        per_focus = jnp.zeros((nfocus, half), F32)
        for j in range(ndose):
            s = s + v[j * nfocus : (j + 1) * nfocus, :] * drow[j : j + 1, here]
            per_focus = per_focus + n[j * nfocus : (j + 1) * nfocus, :]
        srow[:, here] = s + 0.5 * jnp.sum(per_focus, axis=1, keepdims=True) * frow[:, here]
        right = pl.ds(m * 256, cols - m * 256)
        left = jnp.concatenate([srow[:, here], frow[:, here]], axis=0)
        gram[here, right] = full(left, jnp.concatenate([frow[:, right], srow[:, right]], axis=0), TN)

    lane = lax.broadcasted_iota(jnp.int32, (256, 128), 1)
    unroll = 4

    def table_terms(m):
        here = pl.ds(m * 256, 256)

        def dose(step, _):
            left = []
            for e in range(unroll):
                j = step * unroll + e
                at = pl.multiple_of(core * 256 + j * nfocus, nfocus)
                nj = jnp.concatenate(
                    [jnp.sum(counts[pl.ds(at + h * 128, nfocus), :], axis=0, keepdims=True) for h in range(2)], axis=1
                )
                dj = jnp.sum(jnp.where(lane == j, dcol[here, :], 0.0), axis=1, keepdims=True)
                left.append(split(ct[here, :] * nj * dj))
            for r in range(m, 2):
                right = pl.ds(r * 256, 256)
                total = gram[here, right]
                for e, (uh, ul) in enumerate(left):
                    part = dot(uh, ch[mine, right]) + dot(uh, cl[mine, right]) + dot(ul, ch[mine, right])
                    total = total + part * drow[pl.ds(step * unroll + e, 1), right]
                gram[here, right] = total
            return 0

        lax.fori_loop(0, ndose // unroll, dose, 0)
        right = pl.ds(m * 256, cols - m * 256)
        swap = remote(16 + m, gram.at[here, right], gram_twin.at[here, right], twin)
        swap.start()
        return swap

    arrived(3, mate)
    prepare(1)
    swap_counts.wait()
    counts[mine_counts, :] += counts_twin[...]
    focus_terms(1)
    swaps = [(1, table_terms(1))]
    arrived(4, 0)
    arrived(5, 1)
    prepare(0)
    focus_terms(0)
    swaps.append((0, table_terms(0)))

    theirs = pl.ds(pl.multiple_of((1 - core) * half, 128), half)
    for n, slot in ((12, mate), (13, 0), (14, 1)):
        remote(n, c_ref.at[theirs], cs.at[slot, theirs], twin).wait_recv()
    for p in range(4):
        halve(p, theirs)
    outs = [
        pltpu.make_async_copy(source, target, out_sem.at[n])
        for n, (source, target) in enumerate(((ch, ch_out), (cl, cl_out), (ds, ds_out), (fs, fs_out)))
    ]
    for out in outs:
        out.start()
    for m, swap in swaps:
        swap.wait()
        here = pl.ds(m * 256, 256)
        right = pl.ds(m * 256, cols - m * 256)
        gram[here, right] += gram_twin[here, right]
        out = pltpu.make_async_copy(gram.at[here, right], gram_out.at[here, right], out_sem.at[4 + m])
        out.start()
        outs.append(out)
    for copy in sent:
        copy.wait_send()
    for out in outs:
        out.wait()


def call_exchange(seats, clip_cache, dose_scale, focus_term, ids):
    nclip, width = clip_cache.shape
    ndose, nfocus = dose_scale.shape[0], focus_term.shape[0]
    cols = 4 * width
    out = [((nclip, cols), BF16)] * 2 + [((4, ndose, width), F32), ((4, nfocus, width), F32), ((cols, cols), F32)]
    return pl.pallas_call(
        functools.partial(exchange, seats),
        out_shape=[jax.ShapeDtypeStruct(*o) for o in out],
        in_specs=[ANY] * 6,
        out_specs=[ANY] * 5,
        scratch_shapes=[
            pltpu.VMEM((4, nclip, width), F32),
            pltpu.VMEM((4, ndose, width), F32),
            pltpu.VMEM((4, nfocus, width), F32),
        ]
        + [pltpu.VMEM(ids[0].shape, jnp.int32)] * 6
        + [
            pltpu.VMEM((512, 256), F32),
            pltpu.VMEM((256, 256), F32),
            pltpu.VMEM((nclip, cols), BF16),
            pltpu.VMEM((nclip, cols), BF16),
            pltpu.VMEM((cols, nclip // 2), F32),
            pltpu.VMEM((nfocus, cols), F32),
            pltpu.VMEM((nfocus, cols), F32),
            pltpu.VMEM((ndose, cols), F32),
            pltpu.VMEM((cols, 128), F32),
            pltpu.VMEM((cols, cols), F32),
            pltpu.VMEM((cols, cols), F32),
            pltpu.SemaphoreType.DMA((18,)),
            pltpu.SemaphoreType.DMA((18,)),
            pltpu.SemaphoreType.DMA((6,)),
            pltpu.SemaphoreType.DMA((6,)),
        ],
        compiler_params=pltpu.CompilerParams(
            collective_id=0, has_side_effects=True, vmem_limit_bytes=56 * 2**20
        ),
        name="exchange",
    )(clip_cache, dose_scale, focus_term, *ids)


def compute(
    total, ch_in, cl_in, ds_in, fs_in, gram_in, clips_in, doses_in, focuses_in, out,
    ch, cl, ds, fs, gram, clips, doses, focuses, place, where0, where1, where2, where3, sem, where_sem,
    dcol, table, wd, state, rows, out_sem,
):
    where = (where0, where1, where2, where3)
    pairs = (clips_in, clips), (doses_in, doses), (focuses_in, focuses), (gram_in, gram), (fs_in, fs), (ds_in, ds)
    pairs += (ch_in, ch), (cl_in, cl)
    copies = [pltpu.make_async_copy(source, target, sem.at[n]) for n, (source, target) in enumerate(pairs)]
    for copy in copies:
        copy.start()
    nclip, cols = ch.shape
    ndose, nfocus = ds.shape[1], fs.shape[1]
    for copy in copies[:3]:
        copy.wait()
    place[...] = doses[...] * nclip + clips[...]
    for e in range(len(where)):
        pltpu.make_async_copy(place.at[pl.ds(e * where[e].shape[0], where[e].shape[0]), :], where[e], where_sem.at[e]).start()
    for copy in copies[3:6]:
        copy.wait()
    fall = jnp.concatenate([fs[p] for p in range(4)], axis=1)
    for p in range(4):
        dcol[p * 128 : (p + 1) * 128, :] = jnp.concatenate([ds[p], jnp.zeros((128 - ndose, 128), F32)], axis=0).T

    row_i = lax.broadcasted_iota(jnp.int32, (128, 128), 0)
    col_i = lax.broadcasted_iota(jnp.int32, (128, 128), 1)
    squares = jnp.concatenate(
        [
            jnp.sum(jnp.where(row_i == col_i, gram[p * 128 : (p + 1) * 128, p * 128 : (p + 1) * 128], 0.0), axis=0, keepdims=True)
            for p in range(4)
        ],
        axis=1,
    )
    inverse_norm = 1.0 / jnp.sqrt(squares / total + EPSILON)
    norm_col = column(inverse_norm)
    d = squares * inverse_norm * inverse_norm
    d_col = column(d)
    g_prev = gram[:256, :256] * norm_col[:256] * inverse_norm[:, :256]
    g_cross = gram[:256, 256:] * norm_col[:256] * inverse_norm[:, 256:]
    g_own = gram[256:, 256:] * norm_col[256:] * inverse_norm[:, 256:]
    b_prev = 0.5 * g_prev[:128, 128:] / (d_col[:128] + d[:, 128:256])
    b_own = 0.5 * g_own[:128, 128:] / (d_col[256:384] + d[:, 384:])
    (m_prev, m_own), eye = inverses([b_prev, b_own], state)
    z = 2.0 * good(m_prev, b_prev)
    q_right = jnp.concatenate([z, eye - good(b_prev, z, TN)], axis=0)
    q_left = jnp.concatenate([2.0 * m_own - eye, -2.0 * good(b_own, m_own, TN)], axis=0)

    cross = good(good(q_right, g_cross, TN), q_left)
    d_left = jnp.sum(q_right * good(g_prev, q_right), axis=0, keepdims=True)
    d_right = jnp.sum(q_left * good(g_own, q_left), axis=0, keepdims=True)
    b = 0.5 * cross / (column(d_left) + d_right)
    (m,), _ = inverses([b], state)
    z = 2.0 * good(m, b)
    odd = lax.axis_index("panel") % 2 == 1
    top = jnp.where(odd, z, 2.0 * m - eye)
    bottom = jnp.where(odd, eye - good(b, z, TN), -2.0 * good(b, m, TN))
    w = jnp.concatenate([good(q_right, top), good(q_left, bottom)], axis=0) * norm_col
    wd[...] = w

    parts = jnp.concatenate(three(full(fall, w)), axis=0)
    setting = lax.broadcasted_iota(jnp.int32, (3 * nfocus, 128), 0) % nfocus

    def focus(step, _):
        for u in range(8):
            r = step * 8 + u
            chosen = jnp.where(setting == focuses[pl.ds(r, 1), :], 1.0, 0.0).astype(BF16)
            rows[pl.ds(pl.multiple_of(r * 128, 128), 128), :] = dot(chosen, parts, TN)
        return 0

    lax.fori_loop(0, focuses.shape[0] // 8, focus, 0)

    for copy in copies[6:]:
        copy.wait()
    lane = lax.broadcasted_iota(jnp.int32, (cols, 128), 1)

    def rows_of(pair, _):
        scaled = []
        for e in range(2):
            dj = jnp.sum(jnp.where(lane == pair * 2 + e, dcol[...], 0.0), axis=1, keepdims=True)
            scaled.append(wd[...] * dj)
        wh, wl = split(jnp.concatenate(scaled, axis=1))
        for m in range(nclip // 256):
            here = pl.ds(m * 256, 256)
            part = dot(ch[here, :], wh) + dot(cl[here, :], wh) + dot(ch[here, :], wl)
            for e in range(2):
                begin = pl.multiple_of((pair * 2 + e) * nclip + m * 256, 256)
                table[pl.ds(begin, 256), :] = part[:, e * 128 : (e + 1) * 128]
        return 0

    lax.fori_loop(0, ndose // 4, lambda q, c: rows_of(q * 2 + 1, rows_of(q * 2, c)), 0)

    windows = len(where)
    lines = where[0].shape[0]
    steps = place.shape[0] // (windows * lines)
    height = lines * 128

    def window(step, e):
        begin = pl.multiple_of((step * windows + e) * lines, lines)
        return pltpu.make_async_copy(place.at[pl.ds(begin, lines), :], where[e], where_sem.at[e])

    def written(step, e):
        here = pl.ds(pl.multiple_of((step * windows + e) * height, height), height)
        return pltpu.make_async_copy(rows.at[here, :], out.at[here, :], out_sem.at[e])

    def gather(step, _):
        for e in range(windows):
            window(step, e).wait()
            begin = pl.multiple_of((step * windows + e) * height, height)
            for u in range(height // 8):
                found = jnp.concatenate(
                    [table[pl.ds(where[e][u // 16, u % 16 * 8 + r], 1), :] for r in range(8)], axis=0
                )
                here = pl.ds(begin + u * 8, 8)
                rows[here, :] = rows[here, :] + found

            @pl.when(step + 1 < steps)
            def _(e=e):
                window(step + 1, e).start()

            @pl.when(step > 0)
            def _(e=e):
                written(step - 1, e).wait()

            written(step, e).start()
        return 0

    lax.fori_loop(0, steps, gather, 0)
    for e in range(windows):
        written(steps - 1, e).wait()


def call_compute(total, ch, cl, ds, fs, gram, ids):
    lines = ids[0].shape[0]
    nclip, cols = ch.shape
    _, ndose, width = ds.shape
    operands = (ch, cl, ds, fs, gram, *ids)
    return pl.pallas_call(
        functools.partial(compute, float(total)),
        out_shape=jax.ShapeDtypeStruct((lines * 128, width), F32),
        in_specs=[ANY] * 8,
        out_specs=ANY,
        scratch_shapes=[pltpu.VMEM(a.shape, a.dtype) for a in operands]
        + [
            pltpu.VMEM((lines, 128), jnp.int32),
        ]
        + [pltpu.SMEM((4, 128), jnp.int32)] * 4
        + [
            pltpu.SemaphoreType.DMA((8,)),
            pltpu.SemaphoreType.DMA((4,)),
            pltpu.VMEM((cols, 128), F32),
            pltpu.VMEM((ndose * nclip, width), F32),
            pltpu.VMEM((cols, width), F32),
            pltpu.VMEM((2, 2 * width, width), F32),
            pltpu.VMEM((lines * 128, width), F32),
            pltpu.SemaphoreType.DMA((4,)),
        ],
        compiler_params=pltpu.CompilerParams(vmem_limit_bytes=56 * 2**20),
        name="compute",
    )(*operands)


def shards(clip_cache, dose_scale, focus_term, clip_ids, dose_ids, focus_ids):
    rows = clip_ids.shape[0]
    ids = [a.reshape(rows // 128, 128) for a in (clip_ids, dose_ids, focus_ids)]
    gathered = call_exchange(lax.axis_size("panel"), clip_cache, dose_scale, focus_term, ids)
    return call_compute(rows * lax.axis_size("slab"), *gathered, ids)


def solution(mesh):
    return jax.shard_map(
        shards,
        mesh=mesh,
        in_specs=(
            P(None, "panel"),
            P(None, "panel"),
            P(None, "panel"),
            P("slab"),
            P("slab"),
            P("slab"),
        ),
        out_specs=P("slab", "panel"),
        check_vma=False,
    )
```

```python
import functools

import jax
import jax.numpy as jnp
from jax import lax
from jax.experimental import pallas as pl
from jax.experimental.pallas import tpu as pltpu
from jax.sharding import PartitionSpec as P

MESH = pl.DeviceIdType.MESH
EPSILON = 1e-06
F32 = jnp.float32
BF16 = jnp.bfloat16
ANY = pl.BlockSpec(memory_space=pl.ANY)


def split(value):
    high = value.astype(BF16)
    return high, (value - high.astype(F32)).astype(BF16)


def dot(a, b, dims=((1,), (0,))):
    return lax.dot_general(a, b, (dims, ((), ())), preferred_element_type=F32)


def three(value):
    high = value.astype(BF16)
    rest = value - high.astype(F32)
    middle = rest.astype(BF16)
    return high, middle, (rest - middle.astype(F32)).astype(BF16)


def full(a, b, dims=((1,), (0,))):
    a1, a2, a3 = three(a)
    b1, b2, b3 = three(b)
    small = dot(a2, b2, dims) + dot(a1, b3, dims) + dot(a3, b1, dims)
    return dot(a1, b1, dims) + (dot(a1, b2, dims) + dot(a2, b1, dims) + small)


def good(a, b, dims=((1,), (0,))):
    a1, a2 = split(a)
    b1, b2 = split(b)
    return dot(a1, b1, dims) + (dot(a1, b2, dims) + dot(a2, b1, dims))


TN = ((0,), (0,))
NT = ((1,), (1,))


def column(row):
    return jnp.broadcast_to(row, (128, row.shape[1])).T[:, :1]


def inverses(bs, state):
    n = bs[0].shape[0]
    eye = (lax.broadcasted_iota(jnp.int32, (n, n), 0) == lax.broadcasted_iota(jnp.int32, (n, n), 1)).astype(F32)
    squares = [full(b, b, NT) for b in bs]
    bound = functools.reduce(jnp.maximum, [jnp.max(jnp.sum(jnp.abs(s), axis=1)) for s in squares])
    scale = 2.0 / (2.0 + bound)
    for e, s in enumerate(squares):
        rest = (1.0 - scale) * eye - scale * s
        state[e, :n, :] = scale * (eye + rest)
        state[e, n:, :] = full(rest, rest)
    ratio = bound / (2.0 + bound)

    def body(ratio):
        for e in range(len(bs)):
            old = state[e]
            new = full(old, old[n:])
            state[e, :n, :] = old[:n] + new[:n]
            state[e, n:, :] = new[n:]
        return ratio * ratio

    lax.while_loop(lambda ratio: ratio > 1e-8, body, ratio * ratio)
    return [state[e, :n, :] for e in range(len(bs))], eye


def onehot(places, count, offset):
    value = jnp.broadcast_to(places.astype(F32) - offset, (16, places.shape[1])).astype(BF16)
    tile = lax.broadcasted_iota(jnp.int32, (16, places.shape[1]), 0).astype(F32)
    one, none = jnp.ones_like(value), jnp.zeros_like(value)
    return [jnp.where((tile + 16.0 * t).astype(BF16) == value, one, none) for t in range(count // 16)]


def count_ids(counts, clips, doses, focuses):
    rows = 8

    def count(step, _):
        here = pl.ds(pl.multiple_of(step * rows, rows), rows)
        clip = clips[here, :]
        first = (clip // 256) * 128 + doses[here, :] * 8 + focuses[here, :]
        second = clip % 256
        tall, wide = [], []
        for r in range(rows):
            row = first[r : r + 1, :]
            tall.append(jnp.concatenate(onehot(row, 256, 0.0) + onehot(row, 256, 256.0), axis=0))
            wide.append(jnp.concatenate(onehot(second[r : r + 1, :], 256, 0.0), axis=0))
        counts[...] += dot(jnp.concatenate(tall, axis=1), jnp.concatenate(wide, axis=1), NT)
        return 0

    lax.fori_loop(0, clips.shape[0] // rows, count, 0)


def exchange(
    seats, c_ref, d_ref, f_ref, i_ref, j_ref, k_ref, ch_out, cl_out, ds_out, fs_out, gram_out,
    cs, ds, fs, ci, di, fi, oi, oj, ok, counts, counts_twin, ch, cl, ct, frow, srow, drow, dcol, gram, gram_twin, send_sem, recv_sem, local_sem, out_sem,
):
    seat = lax.axis_index("panel")
    slab = lax.axis_index("slab")
    z_hi, core = slab // 2, slab % 2
    side = seat % 2
    base = seat - side
    nclip, width = c_ref.shape
    ndose, nfocus = d_ref.shape[0], f_ref.shape[0]
    cols = 4 * width
    half = nclip // 2

    def near(target):
        z_lo = target % 4
        other = jnp.where((z_lo == 0) | (z_lo == 3), 1, 0)
        return (z_hi + other) % 2

    partner = (seat + 1 - 2 * side, slab)
    next0 = (base + 2) % seats
    next1 = (base + 3) % seats
    to_next0 = (next0, near(next0) * 2 + core)
    to_next1 = (next1, near(next1) * 2 + core)
    from_group = near(seat) * 2 + core
    from_prev0 = ((base + seats - 2) % seats, from_group)
    from_prev1 = ((base + seats - 1) % seats, from_group)
    z_lo = seat % 4
    mirror = (seat - z_lo + 3 - z_lo, (1 - z_hi) * 2 + core)
    twin = (seat, z_hi * 2 + 1 - core)

    own = 2 + side
    pairs = (i_ref, oi), (j_ref, oj), (k_ref, ok), (c_ref, cs.at[own]), (d_ref, ds.at[own]), (f_ref, fs.at[own])
    local = [pltpu.make_async_copy(source, target, local_sem.at[n]) for n, (source, target) in enumerate(pairs)]
    for copy in local:
        copy.start()
    barrier = pltpu.get_barrier_semaphore()
    for device in (partner, from_prev0, from_prev1, mirror, twin):
        pl.semaphore_signal(barrier, inc=1, device_id=device, device_id_type=MESH)
    pl.semaphore_wait(barrier, 5)

    def remote(number, source, target, device, arrival=None):
        return pltpu.make_async_remote_copy(
            src_ref=source,
            dst_ref=target,
            send_sem=send_sem.at[number],
            recv_sem=recv_sem.at[number if arrival is None else arrival],
            device_id=device,
            device_id_type=MESH,
        )

    mine = pl.ds(pl.multiple_of(core * half, 128), half)
    mate = 3 - side
    ids = (i_ref, ci), (j_ref, di), (k_ref, fi)

    sent = []
    for n, (source, target) in enumerate(ids):
        sent.append(remote(n, source, target, mirror))
    sent.append(remote(3, c_ref.at[mine], cs.at[own, mine], partner))
    sent.append(remote(6, d_ref, ds.at[own], partner))
    sent.append(remote(9, f_ref, fs.at[own], partner))
    for n, device in enumerate((to_next0, to_next1)):
        sent.append(remote(4 + n, c_ref.at[mine], cs.at[side, mine], device, 4 + side))
        sent.append(remote(7 + n, d_ref, ds.at[side], device, 7 + side))
        sent.append(remote(10 + n, f_ref, fs.at[side], device, 10 + side))
    for copy in sent:
        copy.start()

    counts[...] = jnp.zeros_like(counts)
    for copy in local:
        copy.wait()
    count_ids(counts, oi, oj, ok)
    for n, (source, target) in enumerate(ids):
        remote(n, source, target, mirror).wait_recv()
    count_ids(counts, ci, di, fi)
    mine_counts = pl.ds(pl.multiple_of(core * 256, 256), 256)
    theirs_counts = pl.ds(pl.multiple_of((1 - core) * 256, 256), 256)
    swap_counts = remote(15, counts.at[theirs_counts], counts_twin, twin)
    swap_counts.start()

    def arrived(n, slot):
        remote(n, c_ref.at[mine], cs.at[slot, mine], partner).wait_recv()
        remote(n + 3, d_ref, ds.at[slot], partner).wait_recv()
        remote(n + 6, f_ref, fs.at[slot], partner).wait_recv()
        forward = remote(9 + n, cs.at[slot, mine], cs.at[slot, mine], twin)
        forward.start()
        sent.append(forward)

    def halve(p, rows):
        high, low = split(cs[p, rows, :])
        ch[rows, p * width : (p + 1) * width] = high
        cl[rows, p * width : (p + 1) * width] = low

    def prepare(m):
        for p in (2 * m, 2 * m + 1):
            halve(p, mine)
            lanes = pl.ds(p * width, width)
            ct[lanes, :] = cs[p, mine, :].T
            frow[:, lanes] = fs[p]
            drow[:, lanes] = ds[p]
            dcol[lanes, :] = jnp.concatenate([ds[p], jnp.zeros((128 - ndose, width), F32)], axis=0).T

    def focus_terms(m):
        here = pl.ds(m * 256, 256)
        right = pl.ds(256, 256)
        n = jnp.concatenate([counts[pl.ds(pl.multiple_of(core * 256 + h * 128, 128), 128), :] for h in range(2)], axis=1)
        nh, nl = split(n)
        v = dot(nh, ch[mine, here]) + dot(nh, cl[mine, here]) + dot(nl, ch[mine, here])
        s = jnp.zeros((nfocus, 256), F32)
        per_focus = jnp.zeros((nfocus, half), F32)
        for j in range(ndose):
            s = s + v[j * nfocus : (j + 1) * nfocus, :] * drow[j : j + 1, here]
            per_focus = per_focus + n[j * nfocus : (j + 1) * nfocus, :]
        srow[:, here] = s + 0.5 * jnp.sum(per_focus, axis=1, keepdims=True) * frow[:, here]
        left = jnp.concatenate([srow[:, here], frow[:, here]], axis=0)
        gram[here, right] = full(left, jnp.concatenate([frow[:, right], srow[:, right]], axis=0), TN)

    lane = lax.broadcasted_iota(jnp.int32, (256, 128), 1)
    right = pl.ds(256, 256)
    unroll = 4

    def table_terms(m):
        here = pl.ds(m * 256, 256)

        def dose(step, _):
            left = []
            for e in range(unroll):
                j = step * unroll + e
                at = pl.multiple_of(core * 256 + j * nfocus, nfocus)
                nj = jnp.concatenate(
                    [jnp.sum(counts[pl.ds(at + h * 128, nfocus), :], axis=0, keepdims=True) for h in range(2)], axis=1
                )
                dj = jnp.sum(jnp.where(lane == j, dcol[here, :], 0.0), axis=1, keepdims=True)
                left.append(split(ct[here, :] * nj * dj))
            total = gram[here, right]
            for e, (uh, ul) in enumerate(left):
                part = dot(uh, ch[mine, right]) + dot(uh, cl[mine, right]) + dot(ul, ch[mine, right])
                total = total + part * drow[pl.ds(step * unroll + e, 1), right]
            gram[here, right] = total
            return 0

        lax.fori_loop(0, ndose // unroll, dose, 0)
        swap = remote(16 + m, gram.at[here, right], gram_twin.at[here, right], twin)
        swap.start()
        return swap

    arrived(3, mate)
    prepare(1)
    swap_counts.wait()
    counts[mine_counts, :] += counts_twin[...]
    focus_terms(1)
    swap_own = table_terms(1)
    arrived(4, 0)
    arrived(5, 1)
    prepare(0)
    focus_terms(0)
    swap_own.wait()
    gram[right, right] += gram_twin[right, right]
    target = (base + 3 - side) % seats
    sent.append(
        remote(
            18,
            gram.at[pl.ds(pl.multiple_of(256 + core * 128, 128), 128), right],
            gram.at[pl.ds(pl.multiple_of(core * 128, 128), 128), pl.ds(0, 256)],
            (target, near(target) * 2 + core),
        )
    )
    sent[-1].start()
    swap_cross = table_terms(0)

    here = pl.ds(0, 256)
    half_rows = gram.at[pl.ds(pl.multiple_of(core * 128, 128), 128), here]
    remote(18, half_rows, half_rows, twin).wait_recv()
    sent.append(remote(19, half_rows, half_rows, twin))
    sent[-1].start()
    theirs = pl.ds(pl.multiple_of((1 - core) * half, 128), half)
    for n, slot in ((12, mate), (13, 0), (14, 1)):
        remote(n, c_ref.at[theirs], cs.at[slot, theirs], twin).wait_recv()
    for p in range(4):
        halve(p, theirs)
    places = ((ch, ch_out), (cl, cl_out), (ds, ds_out), (fs, fs_out))
    outs = [pltpu.make_async_copy(source, target, out_sem.at[n]) for n, (source, target) in enumerate(places)]
    outs.append(pltpu.make_async_copy(gram.at[right, right], gram_out.at[right, right], out_sem.at[4]))
    for out in outs:
        out.start()
    swap_cross.wait()
    gram[here, right] += gram_twin[here, right]
    other_rows = gram.at[pl.ds(pl.multiple_of((1 - core) * 128, 128), 128), here]
    remote(19, other_rows, other_rows, twin).wait_recv()
    outs.append(pltpu.make_async_copy(gram.at[here, :], gram_out.at[here, :], out_sem.at[5]))
    outs[-1].start()
    for copy in sent:
        copy.wait_send()
    for out in outs:
        out.wait()


def call_exchange(seats, clip_cache, dose_scale, focus_term, ids):
    nclip, width = clip_cache.shape
    ndose, nfocus = dose_scale.shape[0], focus_term.shape[0]
    cols = 4 * width
    out = [((nclip, cols), BF16)] * 2 + [((4, ndose, width), F32), ((4, nfocus, width), F32), ((cols, cols), F32)]
    return pl.pallas_call(
        functools.partial(exchange, seats),
        out_shape=[jax.ShapeDtypeStruct(*o) for o in out],
        in_specs=[ANY] * 6,
        out_specs=[ANY] * 5,
        scratch_shapes=[
            pltpu.VMEM((4, nclip, width), F32),
            pltpu.VMEM((4, ndose, width), F32),
            pltpu.VMEM((4, nfocus, width), F32),
        ]
        + [pltpu.VMEM(ids[0].shape, jnp.int32)] * 6
        + [
            pltpu.VMEM((512, 256), F32),
            pltpu.VMEM((256, 256), F32),
            pltpu.VMEM((nclip, cols), BF16),
            pltpu.VMEM((nclip, cols), BF16),
            pltpu.VMEM((cols, nclip // 2), F32),
            pltpu.VMEM((nfocus, cols), F32),
            pltpu.VMEM((nfocus, cols), F32),
            pltpu.VMEM((ndose, cols), F32),
            pltpu.VMEM((cols, 128), F32),
            pltpu.VMEM((cols, cols), F32),
            pltpu.VMEM((cols, cols), F32),
            pltpu.SemaphoreType.DMA((20,)),
            pltpu.SemaphoreType.DMA((20,)),
            pltpu.SemaphoreType.DMA((6,)),
            pltpu.SemaphoreType.DMA((6,)),
        ],
        compiler_params=pltpu.CompilerParams(
            collective_id=0, has_side_effects=True, vmem_limit_bytes=56 * 2**20
        ),
        name="exchange",
    )(clip_cache, dose_scale, focus_term, *ids)


def compute(
    total, ch_in, cl_in, ds_in, fs_in, gram_in, clips_in, doses_in, focuses_in, out,
    ch, cl, ds, fs, gram, clips, doses, focuses, place, where0, where1, where2, where3, sem, where_sem,
    dcol, table, wd, state, rows, out_sem,
):
    where = (where0, where1, where2, where3)
    pairs = (clips_in, clips), (doses_in, doses), (focuses_in, focuses), (gram_in, gram), (fs_in, fs), (ds_in, ds)
    pairs += (ch_in, ch), (cl_in, cl)
    copies = [pltpu.make_async_copy(source, target, sem.at[n]) for n, (source, target) in enumerate(pairs)]
    for copy in copies:
        copy.start()
    nclip, cols = ch.shape
    ndose, nfocus = ds.shape[1], fs.shape[1]
    for copy in copies[:3]:
        copy.wait()
    place[...] = doses[...] * nclip + clips[...]
    for e in range(len(where)):
        pltpu.make_async_copy(place.at[pl.ds(e * where[e].shape[0], where[e].shape[0]), :], where[e], where_sem.at[e]).start()
    for copy in copies[3:6]:
        copy.wait()
    fall = jnp.concatenate([fs[p] for p in range(4)], axis=1)
    for p in range(4):
        dcol[p * 128 : (p + 1) * 128, :] = jnp.concatenate([ds[p], jnp.zeros((128 - ndose, 128), F32)], axis=0).T

    row_i = lax.broadcasted_iota(jnp.int32, (128, 128), 0)
    col_i = lax.broadcasted_iota(jnp.int32, (128, 128), 1)
    squares = jnp.concatenate(
        [
            jnp.sum(jnp.where(row_i == col_i, gram[p * 128 : (p + 1) * 128, p * 128 : (p + 1) * 128], 0.0), axis=0, keepdims=True)
            for p in range(4)
        ],
        axis=1,
    )
    inverse_norm = 1.0 / jnp.sqrt(squares / total + EPSILON)
    norm_col = column(inverse_norm)
    d = squares * inverse_norm * inverse_norm
    d_col = column(d)
    g_prev = gram[:256, :256] * norm_col[:256] * inverse_norm[:, :256]
    g_cross = gram[:256, 256:] * norm_col[:256] * inverse_norm[:, 256:]
    g_own = gram[256:, 256:] * norm_col[256:] * inverse_norm[:, 256:]
    b_prev = 0.5 * g_prev[:128, 128:] / (d_col[:128] + d[:, 128:256])
    b_own = 0.5 * g_own[:128, 128:] / (d_col[256:384] + d[:, 384:])
    (m_prev, m_own), eye = inverses([b_prev, b_own], state)
    z = 2.0 * good(m_prev, b_prev)
    q_right = jnp.concatenate([z, eye - good(b_prev, z, TN)], axis=0)
    q_left = jnp.concatenate([2.0 * m_own - eye, -2.0 * good(b_own, m_own, TN)], axis=0)

    cross = good(good(q_right, g_cross, TN), q_left)
    d_left = jnp.sum(q_right * good(g_prev, q_right), axis=0, keepdims=True)
    d_right = jnp.sum(q_left * good(g_own, q_left), axis=0, keepdims=True)
    b = 0.5 * cross / (column(d_left) + d_right)
    (m,), _ = inverses([b], state)
    z = 2.0 * good(m, b)
    odd = lax.axis_index("panel") % 2 == 1
    top = jnp.where(odd, z, 2.0 * m - eye)
    bottom = jnp.where(odd, eye - good(b, z, TN), -2.0 * good(b, m, TN))
    w = jnp.concatenate([good(q_right, top), good(q_left, bottom)], axis=0) * norm_col
    wd[...] = w

    parts = jnp.concatenate(three(full(fall, w)), axis=0)
    setting = lax.broadcasted_iota(jnp.int32, (3 * nfocus, 128), 0) % nfocus

    def focus(step, _):
        for u in range(8):
            r = step * 8 + u
            chosen = jnp.where(setting == focuses[pl.ds(r, 1), :], 1.0, 0.0).astype(BF16)
            rows[pl.ds(pl.multiple_of(r * 128, 128), 128), :] = dot(chosen, parts, TN)
        return 0

    lax.fori_loop(0, focuses.shape[0] // 8, focus, 0)

    for copy in copies[6:]:
        copy.wait()
    lane = lax.broadcasted_iota(jnp.int32, (cols, 128), 1)

    def rows_of(pair, _):
        scaled = []
        for e in range(2):
            dj = jnp.sum(jnp.where(lane == pair * 2 + e, dcol[...], 0.0), axis=1, keepdims=True)
            scaled.append(wd[...] * dj)
        wh, wl = split(jnp.concatenate(scaled, axis=1))
        for m in range(nclip // 256):
            here = pl.ds(m * 256, 256)
            part = dot(ch[here, :], wh) + dot(cl[here, :], wh) + dot(ch[here, :], wl)
            for e in range(2):
                begin = pl.multiple_of((pair * 2 + e) * nclip + m * 256, 256)
                table[pl.ds(begin, 256), :] = part[:, e * 128 : (e + 1) * 128]
        return 0

    lax.fori_loop(0, ndose // 4, lambda q, c: rows_of(q * 2 + 1, rows_of(q * 2, c)), 0)

    windows = len(where)
    lines = where[0].shape[0]
    steps = place.shape[0] // (windows * lines)
    height = lines * 128

    def window(step, e):
        begin = pl.multiple_of((step * windows + e) * lines, lines)
        return pltpu.make_async_copy(place.at[pl.ds(begin, lines), :], where[e], where_sem.at[e])

    def written(step, e):
        here = pl.ds(pl.multiple_of((step * windows + e) * height, height), height)
        return pltpu.make_async_copy(rows.at[here, :], out.at[here, :], out_sem.at[e])

    def gather(step, _):
        for e in range(windows):
            window(step, e).wait()
            begin = pl.multiple_of((step * windows + e) * height, height)
            for u in range(height // 8):
                found = jnp.concatenate(
                    [table[pl.ds(where[e][u // 16, u % 16 * 8 + r], 1), :] for r in range(8)], axis=0
                )
                here = pl.ds(begin + u * 8, 8)
                rows[here, :] = rows[here, :] + found

            @pl.when(step + 1 < steps)
            def _(e=e):
                window(step + 1, e).start()

            @pl.when(step > 0)
            def _(e=e):
                written(step - 1, e).wait()

            written(step, e).start()
        return 0

    lax.fori_loop(0, steps, gather, 0)
    for e in range(windows):
        written(steps - 1, e).wait()


def call_compute(total, ch, cl, ds, fs, gram, ids):
    lines = ids[0].shape[0]
    nclip, cols = ch.shape
    _, ndose, width = ds.shape
    operands = (ch, cl, ds, fs, gram, *ids)
    return pl.pallas_call(
        functools.partial(compute, float(total)),
        out_shape=jax.ShapeDtypeStruct((lines * 128, width), F32),
        in_specs=[ANY] * 8,
        out_specs=ANY,
        scratch_shapes=[pltpu.VMEM(a.shape, a.dtype) for a in operands]
        + [
            pltpu.VMEM((lines, 128), jnp.int32),
        ]
        + [pltpu.SMEM((4, 128), jnp.int32)] * 4
        + [
            pltpu.SemaphoreType.DMA((8,)),
            pltpu.SemaphoreType.DMA((4,)),
            pltpu.VMEM((cols, 128), F32),
            pltpu.VMEM((ndose * nclip, width), F32),
            pltpu.VMEM((cols, width), F32),
            pltpu.VMEM((2, 2 * width, width), F32),
            pltpu.VMEM((lines * 128, width), F32),
            pltpu.SemaphoreType.DMA((4,)),
        ],
        compiler_params=pltpu.CompilerParams(vmem_limit_bytes=56 * 2**20),
        name="compute",
    )(*operands)


def shards(clip_cache, dose_scale, focus_term, clip_ids, dose_ids, focus_ids):
    rows = clip_ids.shape[0]
    ids = [a.reshape(rows // 128, 128) for a in (clip_ids, dose_ids, focus_ids)]
    gathered = call_exchange(lax.axis_size("panel"), clip_cache, dose_scale, focus_term, ids)
    return call_compute(rows * lax.axis_size("slab"), *gathered, ids)


def solution(mesh):
    return jax.shard_map(
        shards,
        mesh=mesh,
        in_specs=(
            P(None, "panel"),
            P(None, "panel"),
            P(None, "panel"),
            P("slab"),
            P("slab"),
            P("slab"),
        ),
        out_specs=P("slab", "panel"),
        check_vma=False,
    )
```

```python
import functools

import jax
import jax.numpy as jnp
from jax import lax
from jax.experimental import pallas as pl
from jax.experimental.pallas import tpu as pltpu
from jax.sharding import PartitionSpec as P

MESH = pl.DeviceIdType.MESH
EPSILON = 1e-06
F32 = jnp.float32
BF16 = jnp.bfloat16
ANY = pl.BlockSpec(memory_space=pl.ANY)


def split(value):
    high = value.astype(BF16)
    return high, (value - high.astype(F32)).astype(BF16)


def dot(a, b, dims=((1,), (0,))):
    return lax.dot_general(a, b, (dims, ((), ())), preferred_element_type=F32)


def three(value):
    high = value.astype(BF16)
    rest = value - high.astype(F32)
    middle = rest.astype(BF16)
    return high, middle, (rest - middle.astype(F32)).astype(BF16)


def full(a, b, dims=((1,), (0,))):
    a1, a2, a3 = three(a)
    b1, b2, b3 = three(b)
    small = dot(a2, b2, dims) + dot(a1, b3, dims) + dot(a3, b1, dims)
    return dot(a1, b1, dims) + (dot(a1, b2, dims) + dot(a2, b1, dims) + small)


def good(a, b, dims=((1,), (0,))):
    a1, a2 = split(a)
    b1, b2 = split(b)
    return dot(a1, b1, dims) + (dot(a1, b2, dims) + dot(a2, b1, dims))


TN = ((0,), (0,))
NT = ((1,), (1,))


def column(row):
    return jnp.broadcast_to(row, (128, row.shape[1])).T[:, :1]


def inverses(bs, state):
    n = bs[0].shape[0]
    eye = (lax.broadcasted_iota(jnp.int32, (n, n), 0) == lax.broadcasted_iota(jnp.int32, (n, n), 1)).astype(F32)
    squares = [full(b, b, NT) for b in bs]
    bound = functools.reduce(jnp.maximum, [jnp.max(jnp.sum(jnp.abs(s), axis=1)) for s in squares])
    scale = 2.0 / (2.0 + bound)
    for e, s in enumerate(squares):
        rest = (1.0 - scale) * eye - scale * s
        state[e, :n, :] = scale * (eye + rest)
        state[e, n:, :] = full(rest, rest)
    ratio = bound / (2.0 + bound)

    def body(ratio):
        for e in range(len(bs)):
            old = state[e]
            new = full(old, old[n:])
            state[e, :n, :] = old[:n] + new[:n]
            state[e, n:, :] = new[n:]
        return ratio * ratio

    lax.while_loop(lambda ratio: ratio > 1e-8, body, ratio * ratio)
    return [state[e, :n, :] for e in range(len(bs))], eye


def onehot(places, count, offset):
    value = jnp.broadcast_to(places.astype(F32) - offset, (16, places.shape[1])).astype(BF16)
    tile = lax.broadcasted_iota(jnp.int32, (16, places.shape[1]), 0).astype(F32)
    one, none = jnp.ones_like(value), jnp.zeros_like(value)
    return [jnp.where((tile + 16.0 * t).astype(BF16) == value, one, none) for t in range(count // 16)]


def count_ids(counts, clips, doses, focuses):
    rows = 8

    def part(step):
        here = pl.ds(pl.multiple_of(step * rows, rows), rows)
        clip = clips[here, :]
        first = (clip // 256) * 128 + doses[here, :] * 8 + focuses[here, :]
        second = clip % 256
        tall, wide = [], []
        for r in range(rows):
            row = first[r : r + 1, :]
            tall.append(jnp.concatenate(onehot(row, 256, 0.0) + onehot(row, 256, 256.0), axis=0))
            wide.append(jnp.concatenate(onehot(second[r : r + 1, :], 256, 0.0), axis=0))
        return dot(jnp.concatenate(tall, axis=1), jnp.concatenate(wide, axis=1), NT)

    def count(step, _):
        counts[...] += part(step * 2) + part(step * 2 + 1)
        return 0

    lax.fori_loop(0, clips.shape[0] // rows // 2, count, 0)


def exchange(
    seats, c_ref, d_ref, f_ref, i_ref, j_ref, k_ref, ch_out, cl_out, ds_out, fs_out, gram_out,
    cs, ds, fs, ci, di, fi, oi, oj, ok, counts, counts_twin, ch, cl, ct, frow, srow, drow, dcol, gram, gram_twin, send_sem, recv_sem, local_sem, out_sem,
):
    seat = lax.axis_index("panel")
    slab = lax.axis_index("slab")
    z_hi, core = slab // 2, slab % 2
    side = seat % 2
    base = seat - side
    nclip, width = c_ref.shape
    ndose, nfocus = d_ref.shape[0], f_ref.shape[0]
    cols = 4 * width
    half = nclip // 2

    def near(target):
        z_lo = target % 4
        other = jnp.where((z_lo == 0) | (z_lo == 3), 1, 0)
        return (z_hi + other) % 2

    partner = (seat + 1 - 2 * side, slab)
    next0 = (base + 2) % seats
    next1 = (base + 3) % seats
    to_next0 = (next0, near(next0) * 2 + core)
    to_next1 = (next1, near(next1) * 2 + core)
    from_group = near(seat) * 2 + core
    from_prev0 = ((base + seats - 2) % seats, from_group)
    from_prev1 = ((base + seats - 1) % seats, from_group)
    z_lo = seat % 4
    mirror = (seat - z_lo + 3 - z_lo, (1 - z_hi) * 2 + core)
    twin = (seat, z_hi * 2 + 1 - core)

    own = 2 + side
    pairs = (i_ref, oi), (j_ref, oj), (k_ref, ok), (c_ref, cs.at[own]), (d_ref, ds.at[own]), (f_ref, fs.at[own])
    local = [pltpu.make_async_copy(source, target, local_sem.at[n]) for n, (source, target) in enumerate(pairs)]
    for copy in local:
        copy.start()
    barrier = pltpu.get_barrier_semaphore()
    for device in (partner, from_prev0, from_prev1, mirror, twin):
        pl.semaphore_signal(barrier, inc=1, device_id=device, device_id_type=MESH)
    pl.semaphore_wait(barrier, 5)

    def remote(number, source, target, device, arrival=None):
        return pltpu.make_async_remote_copy(
            src_ref=source,
            dst_ref=target,
            send_sem=send_sem.at[number],
            recv_sem=recv_sem.at[number if arrival is None else arrival],
            device_id=device,
            device_id_type=MESH,
        )

    mine = pl.ds(pl.multiple_of(core * half, 128), half)
    mate = 3 - side
    ids = (i_ref, ci), (j_ref, di), (k_ref, fi)

    sent = []
    for n, (source, target) in enumerate(ids):
        sent.append(remote(n, source, target, mirror))
    sent.append(remote(3, c_ref.at[mine], cs.at[own, mine], partner))
    sent.append(remote(6, d_ref, ds.at[own], partner))
    sent.append(remote(9, f_ref, fs.at[own], partner))
    for n, device in enumerate((to_next0, to_next1)):
        sent.append(remote(4 + n, c_ref.at[mine], cs.at[side, mine], device, 4 + side))
        sent.append(remote(7 + n, d_ref, ds.at[side], device, 7 + side))
        sent.append(remote(10 + n, f_ref, fs.at[side], device, 10 + side))
    for copy in sent:
        copy.start()

    counts[...] = jnp.zeros_like(counts)
    for copy in local:
        copy.wait()
    count_ids(counts, oi, oj, ok)
    for n, (source, target) in enumerate(ids):
        remote(n, source, target, mirror).wait_recv()
    count_ids(counts, ci, di, fi)
    mine_counts = pl.ds(pl.multiple_of(core * 256, 256), 256)
    theirs_counts = pl.ds(pl.multiple_of((1 - core) * 256, 256), 256)
    swap_counts = remote(15, counts.at[theirs_counts], counts_twin, twin)
    swap_counts.start()

    def arrived(n, slot):
        remote(n, c_ref.at[mine], cs.at[slot, mine], partner).wait_recv()
        remote(n + 3, d_ref, ds.at[slot], partner).wait_recv()
        remote(n + 6, f_ref, fs.at[slot], partner).wait_recv()
        forward = remote(9 + n, cs.at[slot, mine], cs.at[slot, mine], twin)
        forward.start()
        sent.append(forward)

    def halve(p, rows):
        high, low = split(cs[p, rows, :])
        ch[rows, p * width : (p + 1) * width] = high
        cl[rows, p * width : (p + 1) * width] = low

    def prepare(m):
        for p in (2 * m, 2 * m + 1):
            halve(p, mine)
            lanes = pl.ds(p * width, width)
            ct[lanes, :] = cs[p, mine, :].T
            frow[:, lanes] = fs[p]
            drow[:, lanes] = ds[p]
            dcol[lanes, :] = jnp.concatenate([ds[p], jnp.zeros((128 - ndose, width), F32)], axis=0).T

    def focus_terms(m):
        here = pl.ds(m * 256, 256)
        right = pl.ds(256, 256)
        n = jnp.concatenate([counts[pl.ds(pl.multiple_of(core * 256 + h * 128, 128), 128), :] for h in range(2)], axis=1)
        nh, nl = split(n)
        v = dot(nh, ch[mine, here]) + dot(nh, cl[mine, here]) + dot(nl, ch[mine, here])
        s = jnp.zeros((nfocus, 256), F32)
        per_focus = jnp.zeros((nfocus, half), F32)
        for j in range(ndose):
            s = s + v[j * nfocus : (j + 1) * nfocus, :] * drow[j : j + 1, here]
            per_focus = per_focus + n[j * nfocus : (j + 1) * nfocus, :]
        srow[:, here] = s + 0.5 * jnp.sum(per_focus, axis=1, keepdims=True) * frow[:, here]
        left = jnp.concatenate([srow[:, here], frow[:, here]], axis=0)
        gram[here, right] = full(left, jnp.concatenate([frow[:, right], srow[:, right]], axis=0), TN)

    lane = lax.broadcasted_iota(jnp.int32, (256, 128), 1)
    right = pl.ds(256, 256)
    unroll, stack = 8, 4

    def table_terms(m):
        here = pl.ds(m * 256, 256)

        def dose(step, _):
            total = gram[here, right]
            for first in range(0, unroll, stack):
                left, outer = [], []
                for e in range(first, first + stack):
                    j = step * unroll + e
                    at = pl.multiple_of(core * 256 + j * nfocus, nfocus)
                    nj = jnp.concatenate(
                        [jnp.sum(counts[pl.ds(at + h * 128, nfocus), :], axis=0, keepdims=True) for h in range(2)],
                        axis=1,
                    )
                    left.append(split(ct[here, :] * nj))
                    dj = jnp.sum(jnp.where(lane == j, dcol[here, :], 0.0), axis=1, keepdims=True)
                    outer.append(dj * drow[pl.ds(j, 1), right])
                uh = jnp.concatenate([high for high, _ in left], axis=0)
                ul = jnp.concatenate([low for _, low in left], axis=0)
                part = dot(uh, ch[mine, right]) + dot(ul, ch[mine, right]) + dot(uh, cl[mine, right])
                for e in range(stack):
                    total = total + part[e * 256 : (e + 1) * 256, :] * outer[e]
            gram[here, right] = total
            return 0

        lax.fori_loop(0, ndose // unroll, dose, 0)
        swap = remote(16 + m, gram.at[here, right], gram_twin.at[here, right], twin)
        swap.start()
        return swap

    arrived(3, mate)
    prepare(1)
    swap_counts.wait()
    counts[mine_counts, :] += counts_twin[...]
    focus_terms(1)
    swap_own = table_terms(1)
    arrived(4, 0)
    arrived(5, 1)
    prepare(0)
    focus_terms(0)
    swap_own.wait()
    gram[right, right] += gram_twin[right, right]
    target = (base + 3 - side) % seats
    sent.append(
        remote(
            18,
            gram.at[pl.ds(pl.multiple_of(256 + core * 128, 128), 128), right],
            gram.at[pl.ds(pl.multiple_of(core * 128, 128), 128), pl.ds(0, 256)],
            (target, near(target) * 2 + core),
        )
    )
    sent[-1].start()
    swap_cross = table_terms(0)

    here = pl.ds(0, 256)
    half_rows = gram.at[pl.ds(pl.multiple_of(core * 128, 128), 128), here]
    remote(18, half_rows, half_rows, twin).wait_recv()
    sent.append(remote(19, half_rows, half_rows, twin))
    sent[-1].start()
    theirs = pl.ds(pl.multiple_of((1 - core) * half, 128), half)
    for n, slot in ((12, mate), (13, 0), (14, 1)):
        remote(n, c_ref.at[theirs], cs.at[slot, theirs], twin).wait_recv()
    for p in range(4):
        halve(p, theirs)
    places = ((ch, ch_out), (cl, cl_out), (ds, ds_out), (fs, fs_out))
    outs = [pltpu.make_async_copy(source, target, out_sem.at[n]) for n, (source, target) in enumerate(places)]
    outs.append(pltpu.make_async_copy(gram.at[right, right], gram_out.at[right, right], out_sem.at[4]))
    for out in outs:
        out.start()
    swap_cross.wait()
    gram[here, right] += gram_twin[here, right]
    other_rows = gram.at[pl.ds(pl.multiple_of((1 - core) * 128, 128), 128), here]
    remote(19, other_rows, other_rows, twin).wait_recv()
    outs.append(pltpu.make_async_copy(gram.at[here, :], gram_out.at[here, :], out_sem.at[5]))
    outs[-1].start()
    for copy in sent:
        copy.wait_send()
    for out in outs:
        out.wait()


def call_exchange(seats, clip_cache, dose_scale, focus_term, ids):
    nclip, width = clip_cache.shape
    ndose, nfocus = dose_scale.shape[0], focus_term.shape[0]
    cols = 4 * width
    out = [((nclip, cols), BF16)] * 2 + [((4, ndose, width), F32), ((4, nfocus, width), F32), ((cols, cols), F32)]
    return pl.pallas_call(
        functools.partial(exchange, seats),
        out_shape=[jax.ShapeDtypeStruct(*o) for o in out],
        in_specs=[ANY] * 6,
        out_specs=[ANY] * 5,
        scratch_shapes=[
            pltpu.VMEM((4, nclip, width), F32),
            pltpu.VMEM((4, ndose, width), F32),
            pltpu.VMEM((4, nfocus, width), F32),
        ]
        + [pltpu.VMEM(ids[0].shape, jnp.int32)] * 6
        + [
            pltpu.VMEM((512, 256), F32),
            pltpu.VMEM((256, 256), F32),
            pltpu.VMEM((nclip, cols), BF16),
            pltpu.VMEM((nclip, cols), BF16),
            pltpu.VMEM((cols, nclip // 2), F32),
            pltpu.VMEM((nfocus, cols), F32),
            pltpu.VMEM((nfocus, cols), F32),
            pltpu.VMEM((ndose, cols), F32),
            pltpu.VMEM((cols, 128), F32),
            pltpu.VMEM((cols, cols), F32),
            pltpu.VMEM((cols, cols), F32),
            pltpu.SemaphoreType.DMA((20,)),
            pltpu.SemaphoreType.DMA((20,)),
            pltpu.SemaphoreType.DMA((6,)),
            pltpu.SemaphoreType.DMA((6,)),
        ],
        compiler_params=pltpu.CompilerParams(
            collective_id=0, has_side_effects=True, vmem_limit_bytes=56 * 2**20
        ),
        name="exchange",
    )(clip_cache, dose_scale, focus_term, *ids)


def compute(
    total, ch_in, cl_in, ds_in, fs_in, gram_in, clips_in, doses_in, focuses_in, out,
    ch, cl, ds, fs, gram, clips, doses, focuses, place, where0, where1, where2, where3, sem, where_sem,
    dcol, table, wd, state, rows, out_sem,
):
    where = (where0, where1, where2, where3)
    pairs = (clips_in, clips), (doses_in, doses), (focuses_in, focuses), (gram_in, gram), (fs_in, fs), (ds_in, ds)
    pairs += (ch_in, ch), (cl_in, cl)
    copies = [pltpu.make_async_copy(source, target, sem.at[n]) for n, (source, target) in enumerate(pairs)]
    for copy in copies:
        copy.start()
    nclip, cols = ch.shape
    ndose, nfocus = ds.shape[1], fs.shape[1]
    for copy in copies[:3]:
        copy.wait()
    place[...] = doses[...] * nclip + clips[...]
    for e in range(len(where)):
        pltpu.make_async_copy(place.at[pl.ds(e * where[e].shape[0], where[e].shape[0]), :], where[e], where_sem.at[e]).start()
    for copy in copies[3:6]:
        copy.wait()
    fall = jnp.concatenate([fs[p] for p in range(4)], axis=1)
    for p in range(4):
        dcol[p * 128 : (p + 1) * 128, :] = jnp.concatenate([ds[p], jnp.zeros((128 - ndose, 128), F32)], axis=0).T

    row_i = lax.broadcasted_iota(jnp.int32, (128, 128), 0)
    col_i = lax.broadcasted_iota(jnp.int32, (128, 128), 1)
    squares = jnp.concatenate(
        [
            jnp.sum(jnp.where(row_i == col_i, gram[p * 128 : (p + 1) * 128, p * 128 : (p + 1) * 128], 0.0), axis=0, keepdims=True)
            for p in range(4)
        ],
        axis=1,
    )
    inverse_norm = 1.0 / jnp.sqrt(squares / total + EPSILON)
    norm_col = column(inverse_norm)
    d = squares * inverse_norm * inverse_norm
    d_col = column(d)
    g_prev = gram[:256, :256] * norm_col[:256] * inverse_norm[:, :256]
    g_cross = gram[:256, 256:] * norm_col[:256] * inverse_norm[:, 256:]
    g_own = gram[256:, 256:] * norm_col[256:] * inverse_norm[:, 256:]
    b_prev = 0.5 * g_prev[:128, 128:] / (d_col[:128] + d[:, 128:256])
    b_own = 0.5 * g_own[:128, 128:] / (d_col[256:384] + d[:, 384:])
    (m_prev, m_own), eye = inverses([b_prev, b_own], state)
    z = 2.0 * good(m_prev, b_prev)
    q_right = jnp.concatenate([z, eye - good(b_prev, z, TN)], axis=0)
    q_left = jnp.concatenate([2.0 * m_own - eye, -2.0 * good(b_own, m_own, TN)], axis=0)

    cross = good(good(q_right, g_cross, TN), q_left)
    d_left = jnp.sum(q_right * good(g_prev, q_right), axis=0, keepdims=True)
    d_right = jnp.sum(q_left * good(g_own, q_left), axis=0, keepdims=True)
    b = 0.5 * cross / (column(d_left) + d_right)
    (m,), _ = inverses([b], state)
    z = 2.0 * good(m, b)
    odd = lax.axis_index("panel") % 2 == 1
    top = jnp.where(odd, z, 2.0 * m - eye)
    bottom = jnp.where(odd, eye - good(b, z, TN), -2.0 * good(b, m, TN))
    w = jnp.concatenate([good(q_right, top), good(q_left, bottom)], axis=0) * norm_col
    wd[...] = w

    parts = jnp.concatenate(three(full(fall, w)), axis=0)
    setting = lax.broadcasted_iota(jnp.int32, (3 * nfocus, 128), 0) % nfocus

    for copy in copies[6:]:
        copy.wait()
    lane = lax.broadcasted_iota(jnp.int32, (cols, 128), 1)

    height = 512

    def rows_of(pair, _):
        scaled = []
        for e in range(2):
            dj = jnp.sum(jnp.where(lane == pair * 2 + e, dcol[...], 0.0), axis=1, keepdims=True)
            scaled.append(wd[...] * dj)
        wh, wl = split(jnp.concatenate(scaled, axis=1))
        for m in range(nclip // height):
            here = pl.ds(m * height, height)
            part = dot(ch[here, :], wh) + dot(cl[here, :], wh) + dot(ch[here, :], wl)
            for e in range(2):
                begin = pl.multiple_of((pair * 2 + e) * nclip + m * height, height)
                table[pl.ds(begin, height), :] = part[:, e * 128 : (e + 1) * 128]
        return 0

    lax.fori_loop(0, ndose // 4, lambda q, c: rows_of(q * 2 + 1, rows_of(q * 2, c)), 0)

    windows = len(where)
    lines = where[0].shape[0]
    steps = place.shape[0] // (windows * lines)
    height = lines * 128

    def window(step, e):
        begin = pl.multiple_of((step * windows + e) * lines, lines)
        return pltpu.make_async_copy(place.at[pl.ds(begin, lines), :], where[e], where_sem.at[e])

    def written(step, e):
        here = pl.ds(pl.multiple_of((step * windows + e) * height, height), height)
        return pltpu.make_async_copy(rows.at[here, :], out.at[here, :], out_sem.at[e])

    def gather(step, _):
        for e in range(windows):
            window(step, e).wait()
            begin = pl.multiple_of((step * windows + e) * height, height)
            for line in range(lines):
                ids = focuses[pl.ds((step * windows + e) * lines + line, 1), :]
                part = dot(jnp.where(setting == ids, 1.0, 0.0).astype(BF16), parts, TN)
                for u in range(0, 128, 8):
                    found = jnp.concatenate([table[pl.ds(where[e][line, u + r], 1), :] for r in range(8)], axis=0)
                    rows[pl.ds(begin + line * 128 + u, 8), :] = part[u : u + 8, :] + found

            @pl.when(step + 1 < steps)
            def _(e=e):
                window(step + 1, e).start()

            @pl.when(step > 0)
            def _(e=e):
                written(step - 1, e).wait()

            written(step, e).start()
        return 0

    lax.fori_loop(0, steps, gather, 0)
    for e in range(windows):
        written(steps - 1, e).wait()


def call_compute(total, ch, cl, ds, fs, gram, ids):
    lines = ids[0].shape[0]
    nclip, cols = ch.shape
    _, ndose, width = ds.shape
    operands = (ch, cl, ds, fs, gram, *ids)
    return pl.pallas_call(
        functools.partial(compute, float(total)),
        out_shape=jax.ShapeDtypeStruct((lines * 128, width), F32),
        in_specs=[ANY] * 8,
        out_specs=ANY,
        scratch_shapes=[pltpu.VMEM(a.shape, a.dtype) for a in operands]
        + [
            pltpu.VMEM((lines, 128), jnp.int32),
        ]
        + [pltpu.SMEM((4, 128), jnp.int32)] * 4
        + [
            pltpu.SemaphoreType.DMA((8,)),
            pltpu.SemaphoreType.DMA((4,)),
            pltpu.VMEM((cols, 128), F32),
            pltpu.VMEM((ndose * nclip, width), F32),
            pltpu.VMEM((cols, width), F32),
            pltpu.VMEM((2, 2 * width, width), F32),
            pltpu.VMEM((lines * 128, width), F32),
            pltpu.SemaphoreType.DMA((4,)),
        ],
        compiler_params=pltpu.CompilerParams(vmem_limit_bytes=56 * 2**20),
        name="compute",
    )(*operands)


def shards(clip_cache, dose_scale, focus_term, clip_ids, dose_ids, focus_ids):
    rows = clip_ids.shape[0]
    ids = [a.reshape(rows // 128, 128) for a in (clip_ids, dose_ids, focus_ids)]
    gathered = call_exchange(lax.axis_size("panel"), clip_cache, dose_scale, focus_term, ids)
    return call_compute(rows * lax.axis_size("slab"), *gathered, ids)


def solution(mesh):
    return jax.shard_map(
        shards,
        mesh=mesh,
        in_specs=(
            P(None, "panel"),
            P(None, "panel"),
            P(None, "panel"),
            P("slab"),
            P("slab"),
            P("slab"),
        ),
        out_specs=P("slab", "panel"),
        check_vma=False,
    )
```

```python
import functools

import jax
import jax.numpy as jnp
from jax import lax
from jax.experimental import pallas as pl
from jax.experimental.pallas import tpu as pltpu
from jax.sharding import PartitionSpec as P

MESH = pl.DeviceIdType.MESH
EPSILON = 1e-06
F32 = jnp.float32
BF16 = jnp.bfloat16
ANY = pl.BlockSpec(memory_space=pl.ANY)


def split(value):
    high = value.astype(BF16)
    return high, (value - high.astype(F32)).astype(BF16)


def dot(a, b, dims=((1,), (0,))):
    return lax.dot_general(a, b, (dims, ((), ())), preferred_element_type=F32)


def three(value):
    high = value.astype(BF16)
    rest = value - high.astype(F32)
    middle = rest.astype(BF16)
    return high, middle, (rest - middle.astype(F32)).astype(BF16)


def full(a, b, dims=((1,), (0,))):
    a1, a2, a3 = three(a)
    b1, b2, b3 = three(b)
    small = dot(a2, b2, dims) + dot(a1, b3, dims) + dot(a3, b1, dims)
    return dot(a1, b1, dims) + (dot(a1, b2, dims) + dot(a2, b1, dims) + small)


def good(a, b, dims=((1,), (0,))):
    a1, a2 = split(a)
    b1, b2 = split(b)
    return dot(a1, b1, dims) + (dot(a1, b2, dims) + dot(a2, b1, dims))


TN = ((0,), (0,))
NT = ((1,), (1,))


def column(row):
    return jnp.broadcast_to(row, (128, row.shape[1])).T[:, :1]


def inverses(bs, state):
    n = bs[0].shape[0]
    eye = (lax.broadcasted_iota(jnp.int32, (n, n), 0) == lax.broadcasted_iota(jnp.int32, (n, n), 1)).astype(F32)
    squares = [full(b, b, NT) for b in bs]
    bound = functools.reduce(jnp.maximum, [jnp.max(jnp.sum(jnp.abs(s), axis=1)) for s in squares])
    scale = 2.0 / (2.0 + bound)
    for e, s in enumerate(squares):
        rest = (1.0 - scale) * eye - scale * s
        state[e, :n, :] = scale * (eye + rest)
        state[e, n:, :] = full(rest, rest)
    ratio = bound / (2.0 + bound)

    def body(ratio):
        for e in range(len(bs)):
            old = state[e]
            new = full(old, old[n:])
            state[e, :n, :] = old[:n] + new[:n]
            state[e, n:, :] = new[n:]
        return ratio * ratio

    lax.while_loop(lambda ratio: ratio > 1e-8, body, ratio * ratio)
    return [state[e, :n, :] for e in range(len(bs))], eye


def onehot(places, count, offset):
    value = jnp.broadcast_to(places.astype(F32) - offset, (16, places.shape[1])).astype(BF16)
    tile = lax.broadcasted_iota(jnp.int32, (16, places.shape[1]), 0).astype(F32)
    one, none = jnp.ones_like(value), jnp.zeros_like(value)
    return [jnp.where((tile + 16.0 * t).astype(BF16) == value, one, none) for t in range(count // 16)]


def count_ids(counts, clips, doses, focuses):
    rows = 8

    def part(step):
        here = pl.ds(pl.multiple_of(step * rows, rows), rows)
        clip = clips[here, :]
        first = (clip // 256) * 128 + doses[here, :] * 8 + focuses[here, :]
        second = clip % 256
        tall, wide = [], []
        for r in range(rows):
            row = first[r : r + 1, :]
            tall.append(jnp.concatenate(onehot(row, 256, 0.0) + onehot(row, 256, 256.0), axis=0))
            wide.append(jnp.concatenate(onehot(second[r : r + 1, :], 256, 0.0), axis=0))
        return dot(jnp.concatenate(tall, axis=1), jnp.concatenate(wide, axis=1), NT)

    def count(step, _):
        counts[...] += part(step * 2) + part(step * 2 + 1)
        return 0

    lax.fori_loop(0, clips.shape[0] // rows // 2, count, 0)


def exchange(
    seats, c_ref, d_ref, f_ref, i_ref, j_ref, k_ref, ch_out, cl_out, ds_out, fs_out, gram_out,
    cs, ds, fs, ci, di, fi, oi, oj, ok, counts, counts_twin, ch, cl, ct, frow, srow, drow, dcol, gram, gram_twin, send_sem, recv_sem, local_sem, out_sem,
):
    seat = lax.axis_index("panel")
    slab = lax.axis_index("slab")
    z_hi, core = slab // 2, slab % 2
    side = seat % 2
    base = seat - side
    nclip, width = c_ref.shape
    ndose, nfocus = d_ref.shape[0], f_ref.shape[0]
    cols = 4 * width
    half = nclip // 2

    def near(target):
        z_lo = target % 4
        other = jnp.where((z_lo == 0) | (z_lo == 3), 1, 0)
        return (z_hi + other) % 2

    partner = (seat + 1 - 2 * side, slab)
    next0 = (base + 2) % seats
    next1 = (base + 3) % seats
    to_next0 = (next0, near(next0) * 2 + core)
    to_next1 = (next1, near(next1) * 2 + core)
    from_group = near(seat) * 2 + core
    from_prev0 = ((base + seats - 2) % seats, from_group)
    from_prev1 = ((base + seats - 1) % seats, from_group)
    z_lo = seat % 4
    mirror = (seat - z_lo + 3 - z_lo, (1 - z_hi) * 2 + core)
    twin = (seat, z_hi * 2 + 1 - core)

    own = 2 + side
    pairs = (i_ref, oi), (j_ref, oj), (k_ref, ok), (c_ref, cs.at[own]), (d_ref, ds.at[own]), (f_ref, fs.at[own])
    local = [pltpu.make_async_copy(source, target, local_sem.at[n]) for n, (source, target) in enumerate(pairs)]
    for copy in local:
        copy.start()
    barrier = pltpu.get_barrier_semaphore()
    for device in (partner, from_prev0, from_prev1, mirror, twin):
        pl.semaphore_signal(barrier, inc=1, device_id=device, device_id_type=MESH)
    pl.semaphore_wait(barrier, 5)

    def remote(number, source, target, device, arrival=None):
        return pltpu.make_async_remote_copy(
            src_ref=source,
            dst_ref=target,
            send_sem=send_sem.at[number],
            recv_sem=recv_sem.at[number if arrival is None else arrival],
            device_id=device,
            device_id_type=MESH,
        )

    mine = pl.ds(pl.multiple_of(core * half, 128), half)
    mate = 3 - side
    ids = (i_ref, ci), (j_ref, di), (k_ref, fi)

    sent = []
    for n, (source, target) in enumerate(ids):
        sent.append(remote(n, source, target, mirror))
    sent.append(remote(3, c_ref.at[mine], cs.at[own, mine], partner))
    sent.append(remote(6, d_ref, ds.at[own], partner))
    sent.append(remote(9, f_ref, fs.at[own], partner))
    quarter = [pl.ds(pl.multiple_of(core * half + e * half // 2, 128), half // 2) for e in range(2)]
    for n, device in enumerate((to_next0, to_next1)):
        sent.append(remote(4 + n, c_ref.at[quarter[0]], cs.at[side, quarter[0]], device, 4 + side))
        sent.append(remote(7 + n, d_ref, ds.at[side], device, 7 + side))
        sent.append(remote(10 + n, f_ref, fs.at[side], device, 10 + side))
    for n, device in enumerate((to_next0, to_next1)):
        sent.append(remote(20 + n, c_ref.at[quarter[1]], cs.at[side, quarter[1]], device, 20 + side))
    for copy in sent:
        copy.start()

    counts[...] = jnp.zeros_like(counts)
    for copy in local:
        copy.wait()
    count_ids(counts, oi, oj, ok)
    for n, (source, target) in enumerate(ids):
        remote(n, source, target, mirror).wait_recv()
    count_ids(counts, ci, di, fi)
    mine_counts = pl.ds(pl.multiple_of(core * 256, 256), 256)
    theirs_counts = pl.ds(pl.multiple_of((1 - core) * 256, 256), 256)
    swap_counts = remote(15, counts.at[theirs_counts], counts_twin, twin)
    swap_counts.start()

    def settings(n, slot):
        remote(n + 3, d_ref, ds.at[slot], partner).wait_recv()
        remote(n + 6, f_ref, fs.at[slot], partner).wait_recv()

    def arrived(n, slot, rows):
        remote(n, c_ref.at[rows], cs.at[slot, rows], partner).wait_recv()

    def pass_on(n, slot):
        forward = remote(n, cs.at[slot, mine], cs.at[slot, mine], twin)
        forward.start()
        sent.append(forward)

    def halve(p, rows):
        high, low = split(cs[p, rows, :])
        ch[rows, p * width : (p + 1) * width] = high
        cl[rows, p * width : (p + 1) * width] = low

    def prepare(m, rows, clips):
        for p in (2 * m, 2 * m + 1):
            halve(p, rows)
            ct[p * width : (p + 1) * width, clips] = cs[p, rows, :].T

    def prepare_settings(m):
        for p in (2 * m, 2 * m + 1):
            lanes = pl.ds(p * width, width)
            frow[:, lanes] = fs[p]
            drow[:, lanes] = ds[p]
            dcol[lanes, :] = jnp.concatenate([ds[p], jnp.zeros((128 - ndose, width), F32)], axis=0).T

    def focus_terms(m):
        here = pl.ds(m * 256, 256)
        right = pl.ds(256, 256)
        n = jnp.concatenate([counts[pl.ds(pl.multiple_of(core * 256 + h * 128, 128), 128), :] for h in range(2)], axis=1)
        nh, nl = split(n)
        v = dot(nh, ch[mine, here]) + dot(nh, cl[mine, here]) + dot(nl, ch[mine, here])
        s = jnp.zeros((nfocus, 256), F32)
        per_focus = jnp.zeros((nfocus, half), F32)
        for j in range(ndose):
            s = s + v[j * nfocus : (j + 1) * nfocus, :] * drow[j : j + 1, here]
            per_focus = per_focus + n[j * nfocus : (j + 1) * nfocus, :]
        srow[:, here] = s + 0.5 * jnp.sum(per_focus, axis=1, keepdims=True) * frow[:, here]
        left = jnp.concatenate([srow[:, here], frow[:, here]], axis=0)
        gram[here, right] += full(left, jnp.concatenate([frow[:, right], srow[:, right]], axis=0), TN)

    lane = lax.broadcasted_iota(jnp.int32, (256, 128), 1)
    right = pl.ds(256, 256)
    unroll, stack = 8, 4

    def table_terms(m, rows, parts):
        here = pl.ds(m * 256, 256)
        clips = pl.ds(parts[0] * 256, len(parts) * 256)

        def dose(step, _):
            total = gram[here, right]
            for first in range(0, unroll, stack):
                left, outer = [], []
                for e in range(first, first + stack):
                    j = step * unroll + e
                    at = pl.multiple_of(core * 256 + j * nfocus, nfocus)
                    nj = jnp.concatenate(
                        [jnp.sum(counts[pl.ds(at + h * 128, nfocus), :], axis=0, keepdims=True) for h in parts],
                        axis=1,
                    )
                    left.append(split(ct[here, clips] * nj))
                    dj = jnp.sum(jnp.where(lane == j, dcol[here, :], 0.0), axis=1, keepdims=True)
                    outer.append(dj * drow[pl.ds(j, 1), right])
                uh = jnp.concatenate([high for high, _ in left], axis=0)
                ul = jnp.concatenate([low for _, low in left], axis=0)
                part = dot(uh, ch[rows, right]) + dot(ul, ch[rows, right]) + dot(uh, cl[rows, right])
                for e in range(stack):
                    total = total + part[e * 256 : (e + 1) * 256, :] * outer[e]
            gram[here, right] = total
            return 0

        lax.fori_loop(0, ndose // unroll, dose, 0)

    def swap_terms(m):
        here = pl.ds(m * 256, 256)
        swap = remote(16 + m, gram.at[here, right], gram_twin.at[here, right], twin)
        swap.start()
        return swap

    gram[:, right] = jnp.zeros((cols, 256), F32)
    arrived(3, mate, mine)
    settings(3, mate)
    pass_on(12, mate)
    prepare(1, mine, pl.ds(0, half))
    prepare_settings(1)
    swap_counts.wait()
    counts[mine_counts, :] += counts_twin[...]
    focus_terms(1)
    table_terms(1, mine, (0, 1))
    swap_own = swap_terms(1)
    for slot in range(2):
        arrived(4 + slot, slot, quarter[0])
        settings(4 + slot, slot)
    prepare_settings(0)
    prepare(0, quarter[0], pl.ds(0, half // 2))
    swap_own.wait()
    gram[right, right] += gram_twin[right, right]
    target = (base + 3 - side) % seats
    sent.append(
        remote(
            18,
            gram.at[pl.ds(pl.multiple_of(256 + core * 128, 128), 128), right],
            gram.at[pl.ds(pl.multiple_of(core * 128, 128), 128), pl.ds(0, 256)],
            (target, near(target) * 2 + core),
        )
    )
    sent[-1].start()
    table_terms(0, quarter[0], (0,))
    for slot in range(2):
        arrived(20 + slot, slot, quarter[1])
        pass_on(13 + slot, slot)
    prepare(0, quarter[1], pl.ds(half // 2, half // 2))
    focus_terms(0)
    table_terms(0, quarter[1], (1,))
    swap_cross = swap_terms(0)

    here = pl.ds(0, 256)
    half_rows = gram.at[pl.ds(pl.multiple_of(core * 128, 128), 128), here]
    remote(18, half_rows, half_rows, twin).wait_recv()
    sent.append(remote(19, half_rows, half_rows, twin))
    sent[-1].start()
    theirs = pl.ds(pl.multiple_of((1 - core) * half, 128), half)
    for n, slot in ((12, mate), (13, 0), (14, 1)):
        remote(n, c_ref.at[theirs], cs.at[slot, theirs], twin).wait_recv()
    for p in range(4):
        halve(p, theirs)
    places = ((ch, ch_out), (cl, cl_out), (ds, ds_out), (fs, fs_out))
    outs = [pltpu.make_async_copy(source, target, out_sem.at[n]) for n, (source, target) in enumerate(places)]
    outs.append(pltpu.make_async_copy(gram.at[right, right], gram_out.at[right, right], out_sem.at[4]))
    for out in outs:
        out.start()
    swap_cross.wait()
    gram[here, right] += gram_twin[here, right]
    other_rows = gram.at[pl.ds(pl.multiple_of((1 - core) * 128, 128), 128), here]
    remote(19, other_rows, other_rows, twin).wait_recv()
    outs.append(pltpu.make_async_copy(gram.at[here, :], gram_out.at[here, :], out_sem.at[5]))
    outs[-1].start()
    for copy in sent:
        copy.wait_send()
    for out in outs:
        out.wait()


def call_exchange(seats, clip_cache, dose_scale, focus_term, ids):
    nclip, width = clip_cache.shape
    ndose, nfocus = dose_scale.shape[0], focus_term.shape[0]
    cols = 4 * width
    out = [((nclip, cols), BF16)] * 2 + [((4, ndose, width), F32), ((4, nfocus, width), F32), ((cols, cols), F32)]
    return pl.pallas_call(
        functools.partial(exchange, seats),
        out_shape=[jax.ShapeDtypeStruct(*o) for o in out],
        in_specs=[ANY] * 6,
        out_specs=[ANY] * 5,
        scratch_shapes=[
            pltpu.VMEM((4, nclip, width), F32),
            pltpu.VMEM((4, ndose, width), F32),
            pltpu.VMEM((4, nfocus, width), F32),
        ]
        + [pltpu.VMEM(ids[0].shape, jnp.int32)] * 6
        + [
            pltpu.VMEM((512, 256), F32),
            pltpu.VMEM((256, 256), F32),
            pltpu.VMEM((nclip, cols), BF16),
            pltpu.VMEM((nclip, cols), BF16),
            pltpu.VMEM((cols, nclip // 2), F32),
            pltpu.VMEM((nfocus, cols), F32),
            pltpu.VMEM((nfocus, cols), F32),
            pltpu.VMEM((ndose, cols), F32),
            pltpu.VMEM((cols, 128), F32),
            pltpu.VMEM((cols, cols), F32),
            pltpu.VMEM((cols, cols), F32),
            pltpu.SemaphoreType.DMA((22,)),
            pltpu.SemaphoreType.DMA((22,)),
            pltpu.SemaphoreType.DMA((6,)),
            pltpu.SemaphoreType.DMA((6,)),
        ],
        compiler_params=pltpu.CompilerParams(
            collective_id=0, has_side_effects=True, vmem_limit_bytes=56 * 2**20
        ),
        name="exchange",
    )(clip_cache, dose_scale, focus_term, *ids)


def compute(
    total, ch_in, cl_in, ds_in, fs_in, gram_in, clips_in, doses_in, focuses_in, out,
    ch, cl, ds, fs, gram, clips, doses, focuses, place, where0, where1, where2, where3, sem, where_sem,
    dcol, table, wd, state, rows, out_sem,
):
    where = (where0, where1, where2, where3)
    pairs = (clips_in, clips), (doses_in, doses), (focuses_in, focuses), (gram_in, gram), (fs_in, fs), (ds_in, ds)
    pairs += (ch_in, ch), (cl_in, cl)
    copies = [pltpu.make_async_copy(source, target, sem.at[n]) for n, (source, target) in enumerate(pairs)]
    for copy in copies:
        copy.start()
    nclip, cols = ch.shape
    ndose, nfocus = ds.shape[1], fs.shape[1]
    for copy in copies[:3]:
        copy.wait()
    place[...] = doses[...] * nclip + clips[...]
    for e in range(len(where)):
        pltpu.make_async_copy(place.at[pl.ds(e * where[e].shape[0], where[e].shape[0]), :], where[e], where_sem.at[e]).start()
    for copy in copies[3:6]:
        copy.wait()
    fall = jnp.concatenate([fs[p] for p in range(4)], axis=1)
    for p in range(4):
        dcol[p * 128 : (p + 1) * 128, :] = jnp.concatenate([ds[p], jnp.zeros((128 - ndose, 128), F32)], axis=0).T

    row_i = lax.broadcasted_iota(jnp.int32, (128, 128), 0)
    col_i = lax.broadcasted_iota(jnp.int32, (128, 128), 1)
    squares = jnp.concatenate(
        [
            jnp.sum(jnp.where(row_i == col_i, gram[p * 128 : (p + 1) * 128, p * 128 : (p + 1) * 128], 0.0), axis=0, keepdims=True)
            for p in range(4)
        ],
        axis=1,
    )
    inverse_norm = 1.0 / jnp.sqrt(squares / total + EPSILON)
    norm_col = column(inverse_norm)
    d = squares * inverse_norm * inverse_norm
    d_col = column(d)
    g_prev = gram[:256, :256] * norm_col[:256] * inverse_norm[:, :256]
    g_cross = gram[:256, 256:] * norm_col[:256] * inverse_norm[:, 256:]
    g_own = gram[256:, 256:] * norm_col[256:] * inverse_norm[:, 256:]
    b_prev = 0.5 * g_prev[:128, 128:] / (d_col[:128] + d[:, 128:256])
    b_own = 0.5 * g_own[:128, 128:] / (d_col[256:384] + d[:, 384:])
    (m_prev, m_own), eye = inverses([b_prev, b_own], state)
    z = 2.0 * good(m_prev, b_prev)
    q_right = jnp.concatenate([z, eye - good(b_prev, z, TN)], axis=0)
    q_left = jnp.concatenate([2.0 * m_own - eye, -2.0 * good(b_own, m_own, TN)], axis=0)

    cross = good(good(q_right, g_cross, TN), q_left)
    d_left = jnp.sum(q_right * good(g_prev, q_right), axis=0, keepdims=True)
    d_right = jnp.sum(q_left * good(g_own, q_left), axis=0, keepdims=True)
    b = 0.5 * cross / (column(d_left) + d_right)
    (m,), _ = inverses([b], state)
    z = 2.0 * good(m, b)
    odd = lax.axis_index("panel") % 2 == 1
    top = jnp.where(odd, z, 2.0 * m - eye)
    bottom = jnp.where(odd, eye - good(b, z, TN), -2.0 * good(b, m, TN))
    w = jnp.concatenate([good(q_right, top), good(q_left, bottom)], axis=0) * norm_col
    wd[...] = w

    parts = jnp.concatenate(three(full(fall, w)), axis=0)
    setting = lax.broadcasted_iota(jnp.int32, (3 * nfocus, 128), 0) % nfocus

    for copy in copies[6:]:
        copy.wait()
    lane = lax.broadcasted_iota(jnp.int32, (cols, 128), 1)

    height = 512

    def rows_of(pair, _):
        scaled = []
        for e in range(2):
            dj = jnp.sum(jnp.where(lane == pair * 2 + e, dcol[...], 0.0), axis=1, keepdims=True)
            scaled.append(wd[...] * dj)
        wh, wl = split(jnp.concatenate(scaled, axis=1))
        for m in range(nclip // height):
            here = pl.ds(m * height, height)
            part = dot(ch[here, :], wh) + dot(cl[here, :], wh) + dot(ch[here, :], wl)
            for e in range(2):
                begin = pl.multiple_of((pair * 2 + e) * nclip + m * height, height)
                table[pl.ds(begin, height), :] = part[:, e * 128 : (e + 1) * 128]
        return 0

    lax.fori_loop(0, ndose // 4, lambda q, c: rows_of(q * 2 + 1, rows_of(q * 2, c)), 0)

    windows = len(where)
    lines = where[0].shape[0]
    steps = place.shape[0] // (windows * lines)
    height = lines * 128

    def window(step, e):
        begin = pl.multiple_of((step * windows + e) * lines, lines)
        return pltpu.make_async_copy(place.at[pl.ds(begin, lines), :], where[e], where_sem.at[e])

    def written(step, e):
        here = pl.ds(pl.multiple_of((step * windows + e) * height, height), height)
        return pltpu.make_async_copy(rows.at[here, :], out.at[here, :], out_sem.at[e])

    def gather(step, _):
        for e in range(windows):
            window(step, e).wait()
            begin = pl.multiple_of((step * windows + e) * height, height)
            for line in range(lines):
                ids = focuses[pl.ds((step * windows + e) * lines + line, 1), :]
                part = dot(jnp.where(setting == ids, 1.0, 0.0).astype(BF16), parts, TN)
                for u in range(0, 128, 8):
                    found = jnp.concatenate([table[pl.ds(where[e][line, u + r], 1), :] for r in range(8)], axis=0)
                    rows[pl.ds(begin + line * 128 + u, 8), :] = part[u : u + 8, :] + found

            @pl.when(step + 1 < steps)
            def _(e=e):
                window(step + 1, e).start()

            @pl.when(step > 0)
            def _(e=e):
                written(step - 1, e).wait()

            written(step, e).start()
        return 0

    lax.fori_loop(0, steps, gather, 0)
    for e in range(windows):
        written(steps - 1, e).wait()


def call_compute(total, ch, cl, ds, fs, gram, ids):
    lines = ids[0].shape[0]
    nclip, cols = ch.shape
    _, ndose, width = ds.shape
    operands = (ch, cl, ds, fs, gram, *ids)
    return pl.pallas_call(
        functools.partial(compute, float(total)),
        out_shape=jax.ShapeDtypeStruct((lines * 128, width), F32),
        in_specs=[ANY] * 8,
        out_specs=ANY,
        scratch_shapes=[pltpu.VMEM(a.shape, a.dtype) for a in operands]
        + [
            pltpu.VMEM((lines, 128), jnp.int32),
        ]
        + [pltpu.SMEM((4, 128), jnp.int32)] * 4
        + [
            pltpu.SemaphoreType.DMA((8,)),
            pltpu.SemaphoreType.DMA((4,)),
            pltpu.VMEM((cols, 128), F32),
            pltpu.VMEM((ndose * nclip, width), F32),
            pltpu.VMEM((cols, width), F32),
            pltpu.VMEM((2, 2 * width, width), F32),
            pltpu.VMEM((lines * 128, width), F32),
            pltpu.SemaphoreType.DMA((4,)),
        ],
        compiler_params=pltpu.CompilerParams(vmem_limit_bytes=56 * 2**20),
        name="compute",
    )(*operands)


def shards(clip_cache, dose_scale, focus_term, clip_ids, dose_ids, focus_ids):
    rows = clip_ids.shape[0]
    ids = [a.reshape(rows // 128, 128) for a in (clip_ids, dose_ids, focus_ids)]
    gathered = call_exchange(lax.axis_size("panel"), clip_cache, dose_scale, focus_term, ids)
    return call_compute(rows * lax.axis_size("slab"), *gathered, ids)


def solution(mesh):
    return jax.shard_map(
        shards,
        mesh=mesh,
        in_specs=(
            P(None, "panel"),
            P(None, "panel"),
            P(None, "panel"),
            P("slab"),
            P("slab"),
            P("slab"),
        ),
        out_specs=P("slab", "panel"),
        check_vma=False,
    )
```

```python
import functools

import jax
import jax.numpy as jnp
from jax import lax
from jax.experimental import pallas as pl
from jax.experimental.pallas import tpu as pltpu
from jax.sharding import PartitionSpec as P

MESH = pl.DeviceIdType.MESH
EPSILON = 1e-06
F32 = jnp.float32
BF16 = jnp.bfloat16
ANY = pl.BlockSpec(memory_space=pl.ANY)


def split(value):
    high = value.astype(BF16)
    return high, (value - high.astype(F32)).astype(BF16)


def dot(a, b, dims=((1,), (0,))):
    return lax.dot_general(a, b, (dims, ((), ())), preferred_element_type=F32)


def three(value):
    high = value.astype(BF16)
    rest = value - high.astype(F32)
    middle = rest.astype(BF16)
    return high, middle, (rest - middle.astype(F32)).astype(BF16)


def full(a, b, dims=((1,), (0,))):
    a1, a2, a3 = three(a)
    b1, b2, b3 = three(b)
    small = dot(a2, b2, dims) + dot(a1, b3, dims) + dot(a3, b1, dims)
    return dot(a1, b1, dims) + (dot(a1, b2, dims) + dot(a2, b1, dims) + small)


def good(a, b, dims=((1,), (0,))):
    a1, a2 = split(a)
    b1, b2 = split(b)
    return dot(a1, b1, dims) + (dot(a1, b2, dims) + dot(a2, b1, dims))


TN = ((0,), (0,))
NT = ((1,), (1,))


def column(row):
    return jnp.broadcast_to(row, (128, row.shape[1])).T[:, :1]


def inverses(bs, state):
    n = bs[0].shape[0]
    eye = (lax.broadcasted_iota(jnp.int32, (n, n), 0) == lax.broadcasted_iota(jnp.int32, (n, n), 1)).astype(F32)
    squares = [full(b, b, NT) for b in bs]
    bound = functools.reduce(jnp.maximum, [jnp.max(jnp.sum(jnp.abs(s), axis=1)) for s in squares])
    scale = 2.0 / (2.0 + bound)
    for e, s in enumerate(squares):
        rest = (1.0 - scale) * eye - scale * s
        state[e, :n, :] = scale * (eye + rest)
        state[e, n:, :] = full(rest, rest)
    ratio = bound / (2.0 + bound)

    def body(ratio):
        for e in range(len(bs)):
            old = state[e]
            new = full(old, old[n:])
            state[e, :n, :] = old[:n] + new[:n]
            state[e, n:, :] = new[n:]
        return ratio * ratio

    lax.while_loop(lambda ratio: ratio > 1e-8, body, ratio * ratio)
    return [state[e, :n, :] for e in range(len(bs))], eye


def onehot(places, count, offset):
    value = jnp.broadcast_to(places.astype(F32) - offset, (16, places.shape[1])).astype(BF16)
    tile = lax.broadcasted_iota(jnp.int32, (16, places.shape[1]), 0).astype(F32)
    one, none = jnp.ones_like(value), jnp.zeros_like(value)
    return [jnp.where((tile + 16.0 * t).astype(BF16) == value, one, none) for t in range(count // 16)]


def count_ids(counts, clips, doses, focuses):
    rows = 8

    def part(step):
        here = pl.ds(pl.multiple_of(step * rows, rows), rows)
        clip = clips[here, :]
        first = (clip // 256) * 128 + doses[here, :] * 8 + focuses[here, :]
        second = clip % 256
        tall, wide = [], []
        for r in range(rows):
            row = first[r : r + 1, :]
            tall.append(jnp.concatenate(onehot(row, 256, 0.0) + onehot(row, 256, 256.0), axis=0))
            wide.append(jnp.concatenate(onehot(second[r : r + 1, :], 256, 0.0), axis=0))
        return dot(jnp.concatenate(tall, axis=1), jnp.concatenate(wide, axis=1), NT)

    def count(step, _):
        counts[...] += part(step * 2) + part(step * 2 + 1)
        return 0

    lax.fori_loop(0, clips.shape[0] // rows // 2, count, 0)


def exchange(
    seats, c_ref, d_ref, f_ref, i_ref, j_ref, k_ref, ch_out, cl_out, ds_out, fs_out, gram_out,
    cs, ds, fs, ci, di, fi, oi, oj, ok, counts, counts_twin, ch, cl, ct, frow, srow, drow, dcol, gram, gram_twin, send_sem, recv_sem, local_sem, out_sem,
):
    seat = lax.axis_index("panel")
    slab = lax.axis_index("slab")
    z_hi, core = slab // 2, slab % 2
    side = seat % 2
    base = seat - side
    nclip, width = c_ref.shape
    ndose, nfocus = d_ref.shape[0], f_ref.shape[0]
    cols = 4 * width
    half = nclip // 2

    def near(target):
        z_lo = target % 4
        other = jnp.where((z_lo == 0) | (z_lo == 3), 1, 0)
        return (z_hi + other) % 2

    partner = (seat + 1 - 2 * side, slab)
    next0 = (base + 2) % seats
    next1 = (base + 3) % seats
    to_next0 = (next0, near(next0) * 2 + core)
    to_next1 = (next1, near(next1) * 2 + core)
    from_group = near(seat) * 2 + core
    from_prev0 = ((base + seats - 2) % seats, from_group)
    from_prev1 = ((base + seats - 1) % seats, from_group)
    z_lo = seat % 4
    mirror = (seat - z_lo + 3 - z_lo, (1 - z_hi) * 2 + core)
    twin = (seat, z_hi * 2 + 1 - core)

    own = 2 + side
    pairs = (i_ref, oi), (j_ref, oj), (k_ref, ok), (c_ref, cs.at[own]), (d_ref, ds.at[own]), (f_ref, fs.at[own])
    local = [pltpu.make_async_copy(source, target, local_sem.at[n]) for n, (source, target) in enumerate(pairs)]
    for copy in local:
        copy.start()
    barrier = pltpu.get_barrier_semaphore()
    for device in (partner, from_prev0, from_prev1, mirror, twin):
        pl.semaphore_signal(barrier, inc=1, device_id=device, device_id_type=MESH)
    pl.semaphore_wait(barrier, 5)

    def remote(number, source, target, device, arrival=None):
        return pltpu.make_async_remote_copy(
            src_ref=source,
            dst_ref=target,
            send_sem=send_sem.at[number],
            recv_sem=recv_sem.at[number if arrival is None else arrival],
            device_id=device,
            device_id_type=MESH,
        )

    mine = pl.ds(pl.multiple_of(core * half, 128), half)
    mate = 3 - side
    ids = (i_ref, ci), (j_ref, di), (k_ref, fi)

    sent = []
    for n, (source, target) in enumerate(ids):
        sent.append(remote(n, source, target, mirror))
    sent.append(remote(3, c_ref.at[mine], cs.at[own, mine], partner))
    sent.append(remote(6, d_ref, ds.at[own], partner))
    sent.append(remote(9, f_ref, fs.at[own], partner))
    quarter = [pl.ds(pl.multiple_of(core * half + e * half // 2, 128), half // 2) for e in range(2)]
    for n, device in enumerate((to_next0, to_next1)):
        sent.append(remote(4 + n, c_ref.at[quarter[0]], cs.at[side, quarter[0]], device, 4 + side))
        sent.append(remote(7 + n, d_ref, ds.at[side], device, 7 + side))
        sent.append(remote(10 + n, f_ref, fs.at[side], device, 10 + side))
    for n, device in enumerate((to_next0, to_next1)):
        sent.append(remote(20 + n, c_ref.at[quarter[1]], cs.at[side, quarter[1]], device, 20 + side))
    for copy in sent:
        copy.start()

    counts[...] = jnp.zeros_like(counts)
    for copy in local:
        copy.wait()
    count_ids(counts, oi, oj, ok)
    for n, (source, target) in enumerate(ids):
        remote(n, source, target, mirror).wait_recv()
    count_ids(counts, ci, di, fi)
    mine_counts = pl.ds(pl.multiple_of(core * 256, 256), 256)
    theirs_counts = pl.ds(pl.multiple_of((1 - core) * 256, 256), 256)
    swap_counts = remote(15, counts.at[theirs_counts], counts_twin, twin)
    swap_counts.start()

    def settings(n, slot):
        remote(n + 3, d_ref, ds.at[slot], partner).wait_recv()
        remote(n + 6, f_ref, fs.at[slot], partner).wait_recv()

    def arrived(n, slot, rows):
        remote(n, c_ref.at[rows], cs.at[slot, rows], partner).wait_recv()

    def pass_on(n, slot):
        forward = remote(n, cs.at[slot, mine], cs.at[slot, mine], twin)
        forward.start()
        sent.append(forward)

    def halve(p, rows):
        high, low = split(cs[p, rows, :])
        ch[rows, p * width : (p + 1) * width] = high
        cl[rows, p * width : (p + 1) * width] = low

    def prepare(m, rows, clips):
        for p in (2 * m, 2 * m + 1):
            halve(p, rows)
            ct[p * width : (p + 1) * width, clips] = cs[p, rows, :].T

    def prepare_settings(m):
        for p in (2 * m, 2 * m + 1):
            lanes = pl.ds(p * width, width)
            frow[:, lanes] = fs[p]
            drow[:, lanes] = ds[p]
            dcol[lanes, :] = jnp.concatenate([ds[p], jnp.zeros((128 - ndose, width), F32)], axis=0).T

    def focus_terms(m):
        here = pl.ds(m * 256, 256)
        right = pl.ds(256, 256)
        n = jnp.concatenate([counts[pl.ds(pl.multiple_of(core * 256 + h * 128, 128), 128), :] for h in range(2)], axis=1)
        nh, nl = split(n)
        v = dot(nh, ch[mine, here]) + dot(nh, cl[mine, here]) + dot(nl, ch[mine, here])
        s = jnp.zeros((nfocus, 256), F32)
        per_focus = jnp.zeros((nfocus, half), F32)
        for j in range(ndose):
            s = s + v[j * nfocus : (j + 1) * nfocus, :] * drow[j : j + 1, here]
            per_focus = per_focus + n[j * nfocus : (j + 1) * nfocus, :]
        srow[:, here] = s + 0.5 * jnp.sum(per_focus, axis=1, keepdims=True) * frow[:, here]
        left = jnp.concatenate([srow[:, here], frow[:, here]], axis=0)
        gram[here, right] += full(left, jnp.concatenate([frow[:, right], srow[:, right]], axis=0), TN)

    lane = lax.broadcasted_iota(jnp.int32, (256, 128), 1)
    right = pl.ds(256, 256)
    unroll, stack = 8, 4

    def table_terms(m, rows, parts):
        here = pl.ds(m * 256, 256)
        clips = pl.ds(parts[0] * 256, len(parts) * 256)

        def dose(step, _):
            total = gram[here, right]
            for first in range(0, unroll, stack):
                left, outer = [], []
                for e in range(first, first + stack):
                    j = step * unroll + e
                    at = pl.multiple_of(core * 256 + j * nfocus, nfocus)
                    nj = jnp.concatenate(
                        [jnp.sum(counts[pl.ds(at + h * 128, nfocus), :], axis=0, keepdims=True) for h in parts],
                        axis=1,
                    )
                    left.append(split(ct[here, clips] * nj))
                    dj = jnp.sum(jnp.where(lane == j, dcol[here, :], 0.0), axis=1, keepdims=True)
                    outer.append(dj * drow[pl.ds(j, 1), right])
                uh = jnp.concatenate([high for high, _ in left], axis=0)
                ul = jnp.concatenate([low for _, low in left], axis=0)
                part = dot(uh, ch[rows, right]) + dot(ul, ch[rows, right]) + dot(uh, cl[rows, right])
                for e in range(stack):
                    total = total + part[e * 256 : (e + 1) * 256, :] * outer[e]
            gram[here, right] = total
            return 0

        lax.fori_loop(0, ndose // unroll, dose, 0)

    def swap_terms(m):
        here = pl.ds(m * 256, 256)
        swap = remote(16 + m, gram.at[here, right], gram_twin.at[here, right], twin)
        swap.start()
        return swap

    gram[:, right] = jnp.zeros((cols, 256), F32)
    arrived(3, mate, mine)
    settings(3, mate)
    pass_on(12, mate)
    prepare(1, mine, pl.ds(0, half))
    prepare_settings(1)
    swap_counts.wait()
    counts[mine_counts, :] += counts_twin[...]
    focus_terms(1)
    table_terms(1, mine, (0, 1))
    swap_own = swap_terms(1)
    theirs = pl.ds(pl.multiple_of((1 - core) * half, 128), half)
    remote(12, c_ref.at[theirs], cs.at[mate, theirs], twin).wait_recv()
    for p in (2, 3):
        halve(p, theirs)
    early = pl.ds(256, 256)
    outs = [
        pltpu.make_async_copy(source.at[:, early], target.at[:, early], out_sem.at[6 + n])
        for n, (source, target) in enumerate(((ch, ch_out), (cl, cl_out)))
    ]
    for out in outs:
        out.start()
    for slot in range(2):
        arrived(4 + slot, slot, quarter[0])
        settings(4 + slot, slot)
    prepare_settings(0)
    prepare(0, quarter[0], pl.ds(0, half // 2))
    swap_own.wait()
    gram[right, right] += gram_twin[right, right]
    target = (base + 3 - side) % seats
    sent.append(
        remote(
            18,
            gram.at[pl.ds(pl.multiple_of(256 + core * 128, 128), 128), right],
            gram.at[pl.ds(pl.multiple_of(core * 128, 128), 128), pl.ds(0, 256)],
            (target, near(target) * 2 + core),
        )
    )
    sent[-1].start()
    table_terms(0, quarter[0], (0,))
    for slot in range(2):
        arrived(20 + slot, slot, quarter[1])
        pass_on(13 + slot, slot)
    prepare(0, quarter[1], pl.ds(half // 2, half // 2))
    focus_terms(0)
    table_terms(0, quarter[1], (1,))
    swap_cross = swap_terms(0)

    here = pl.ds(0, 256)
    half_rows = gram.at[pl.ds(pl.multiple_of(core * 128, 128), 128), here]
    remote(18, half_rows, half_rows, twin).wait_recv()
    sent.append(remote(19, half_rows, half_rows, twin))
    sent[-1].start()
    for n, slot in ((13, 0), (14, 1)):
        remote(n, c_ref.at[theirs], cs.at[slot, theirs], twin).wait_recv()
    for p in range(2):
        halve(p, theirs)
    late = pl.ds(0, 256)
    places = (ch.at[:, late], ch_out.at[:, late]), (cl.at[:, late], cl_out.at[:, late]), (ds, ds_out), (fs, fs_out)
    rest = [pltpu.make_async_copy(source, target, out_sem.at[n]) for n, (source, target) in enumerate(places)]
    rest.append(pltpu.make_async_copy(gram.at[right, right], gram_out.at[right, right], out_sem.at[4]))
    for out in rest:
        out.start()
    outs.extend(rest)
    swap_cross.wait()
    gram[here, right] += gram_twin[here, right]
    other_rows = gram.at[pl.ds(pl.multiple_of((1 - core) * 128, 128), 128), here]
    remote(19, other_rows, other_rows, twin).wait_recv()
    outs.append(pltpu.make_async_copy(gram.at[here, :], gram_out.at[here, :], out_sem.at[5]))
    outs[-1].start()
    for copy in sent:
        copy.wait_send()
    for out in outs:
        out.wait()


def call_exchange(seats, clip_cache, dose_scale, focus_term, ids):
    nclip, width = clip_cache.shape
    ndose, nfocus = dose_scale.shape[0], focus_term.shape[0]
    cols = 4 * width
    out = [((nclip, cols), BF16)] * 2 + [((4, ndose, width), F32), ((4, nfocus, width), F32), ((cols, cols), F32)]
    return pl.pallas_call(
        functools.partial(exchange, seats),
        out_shape=[jax.ShapeDtypeStruct(*o) for o in out],
        in_specs=[ANY] * 6,
        out_specs=[ANY] * 5,
        scratch_shapes=[
            pltpu.VMEM((4, nclip, width), F32),
            pltpu.VMEM((4, ndose, width), F32),
            pltpu.VMEM((4, nfocus, width), F32),
        ]
        + [pltpu.VMEM(ids[0].shape, jnp.int32)] * 6
        + [
            pltpu.VMEM((512, 256), F32),
            pltpu.VMEM((256, 256), F32),
            pltpu.VMEM((nclip, cols), BF16),
            pltpu.VMEM((nclip, cols), BF16),
            pltpu.VMEM((cols, nclip // 2), F32),
            pltpu.VMEM((nfocus, cols), F32),
            pltpu.VMEM((nfocus, cols), F32),
            pltpu.VMEM((ndose, cols), F32),
            pltpu.VMEM((cols, 128), F32),
            pltpu.VMEM((cols, cols), F32),
            pltpu.VMEM((cols, cols), F32),
            pltpu.SemaphoreType.DMA((22,)),
            pltpu.SemaphoreType.DMA((22,)),
            pltpu.SemaphoreType.DMA((6,)),
            pltpu.SemaphoreType.DMA((8,)),
        ],
        compiler_params=pltpu.CompilerParams(
            collective_id=0, has_side_effects=True, vmem_limit_bytes=56 * 2**20
        ),
        name="exchange",
    )(clip_cache, dose_scale, focus_term, *ids)


def compute(
    total, ch_in, cl_in, ds_in, fs_in, gram_in, clips_in, doses_in, focuses_in, out,
    ch, cl, ds, fs, gram, clips, doses, focuses, place, where0, where1, where2, where3, sem, where_sem,
    dcol, table, wd, state, rows, out_sem,
):
    where = (where0, where1, where2, where3)
    pairs = (clips_in, clips), (doses_in, doses), (focuses_in, focuses), (gram_in, gram), (fs_in, fs), (ds_in, ds)
    pairs += (ch_in, ch), (cl_in, cl)
    copies = [pltpu.make_async_copy(source, target, sem.at[n]) for n, (source, target) in enumerate(pairs)]
    for copy in copies:
        copy.start()
    nclip, cols = ch.shape
    ndose, nfocus = ds.shape[1], fs.shape[1]
    for copy in copies[:3]:
        copy.wait()
    place[...] = doses[...] * nclip + clips[...]
    for e in range(len(where)):
        pltpu.make_async_copy(place.at[pl.ds(e * where[e].shape[0], where[e].shape[0]), :], where[e], where_sem.at[e]).start()
    for copy in copies[3:6]:
        copy.wait()
    fall = jnp.concatenate([fs[p] for p in range(4)], axis=1)
    for p in range(4):
        dcol[p * 128 : (p + 1) * 128, :] = jnp.concatenate([ds[p], jnp.zeros((128 - ndose, 128), F32)], axis=0).T

    row_i = lax.broadcasted_iota(jnp.int32, (128, 128), 0)
    col_i = lax.broadcasted_iota(jnp.int32, (128, 128), 1)
    squares = jnp.concatenate(
        [
            jnp.sum(jnp.where(row_i == col_i, gram[p * 128 : (p + 1) * 128, p * 128 : (p + 1) * 128], 0.0), axis=0, keepdims=True)
            for p in range(4)
        ],
        axis=1,
    )
    inverse_norm = 1.0 / jnp.sqrt(squares / total + EPSILON)
    norm_col = column(inverse_norm)
    d = squares * inverse_norm * inverse_norm
    d_col = column(d)
    g_prev = gram[:256, :256] * norm_col[:256] * inverse_norm[:, :256]
    g_cross = gram[:256, 256:] * norm_col[:256] * inverse_norm[:, 256:]
    g_own = gram[256:, 256:] * norm_col[256:] * inverse_norm[:, 256:]
    b_prev = 0.5 * g_prev[:128, 128:] / (d_col[:128] + d[:, 128:256])
    b_own = 0.5 * g_own[:128, 128:] / (d_col[256:384] + d[:, 384:])
    (m_prev, m_own), eye = inverses([b_prev, b_own], state)
    z = 2.0 * good(m_prev, b_prev)
    q_right = jnp.concatenate([z, eye - good(b_prev, z, TN)], axis=0)
    q_left = jnp.concatenate([2.0 * m_own - eye, -2.0 * good(b_own, m_own, TN)], axis=0)

    cross = good(good(q_right, g_cross, TN), q_left)
    d_left = jnp.sum(q_right * good(g_prev, q_right), axis=0, keepdims=True)
    d_right = jnp.sum(q_left * good(g_own, q_left), axis=0, keepdims=True)
    b = 0.5 * cross / (column(d_left) + d_right)
    (m,), _ = inverses([b], state)
    z = 2.0 * good(m, b)
    odd = lax.axis_index("panel") % 2 == 1
    top = jnp.where(odd, z, 2.0 * m - eye)
    bottom = jnp.where(odd, eye - good(b, z, TN), -2.0 * good(b, m, TN))
    w = jnp.concatenate([good(q_right, top), good(q_left, bottom)], axis=0) * norm_col
    wd[...] = w

    parts = jnp.concatenate(three(full(fall, w)), axis=0)
    setting = lax.broadcasted_iota(jnp.int32, (3 * nfocus, 128), 0) % nfocus

    for copy in copies[6:]:
        copy.wait()
    lane = lax.broadcasted_iota(jnp.int32, (cols, 128), 1)

    height = 512

    def rows_of(pair, _):
        scaled = []
        for e in range(2):
            dj = jnp.sum(jnp.where(lane == pair * 2 + e, dcol[...], 0.0), axis=1, keepdims=True)
            scaled.append(wd[...] * dj)
        wh, wl = split(jnp.concatenate(scaled, axis=1))
        for m in range(nclip // height):
            here = pl.ds(m * height, height)
            part = dot(ch[here, :], wh) + dot(cl[here, :], wh) + dot(ch[here, :], wl)
            for e in range(2):
                begin = pl.multiple_of((pair * 2 + e) * nclip + m * height, height)
                table[pl.ds(begin, height), :] = part[:, e * 128 : (e + 1) * 128]
        return 0

    lax.fori_loop(0, ndose // 4, lambda q, c: rows_of(q * 2 + 1, rows_of(q * 2, c)), 0)

    windows = len(where)
    lines = where[0].shape[0]
    steps = place.shape[0] // (windows * lines)
    height = lines * 128

    def window(step, e):
        begin = pl.multiple_of((step * windows + e) * lines, lines)
        return pltpu.make_async_copy(place.at[pl.ds(begin, lines), :], where[e], where_sem.at[e])

    def written(step, e):
        here = pl.ds(pl.multiple_of((step * windows + e) * height, height), height)
        return pltpu.make_async_copy(rows.at[here, :], out.at[here, :], out_sem.at[e])

    def gather(step, _):
        for e in range(windows):
            window(step, e).wait()
            begin = pl.multiple_of((step * windows + e) * height, height)
            for line in range(lines):
                ids = focuses[pl.ds((step * windows + e) * lines + line, 1), :]
                part = dot(jnp.where(setting == ids, 1.0, 0.0).astype(BF16), parts, TN)
                for u in range(0, 128, 8):
                    found = jnp.concatenate([table[pl.ds(where[e][line, u + r], 1), :] for r in range(8)], axis=0)
                    rows[pl.ds(begin + line * 128 + u, 8), :] = part[u : u + 8, :] + found

            @pl.when(step + 1 < steps)
            def _(e=e):
                window(step + 1, e).start()

            @pl.when(step > 0)
            def _(e=e):
                written(step - 1, e).wait()

            written(step, e).start()
        return 0

    lax.fori_loop(0, steps, gather, 0)
    for e in range(windows):
        written(steps - 1, e).wait()


def call_compute(total, ch, cl, ds, fs, gram, ids):
    lines = ids[0].shape[0]
    nclip, cols = ch.shape
    _, ndose, width = ds.shape
    operands = (ch, cl, ds, fs, gram, *ids)
    return pl.pallas_call(
        functools.partial(compute, float(total)),
        out_shape=jax.ShapeDtypeStruct((lines * 128, width), F32),
        in_specs=[ANY] * 8,
        out_specs=ANY,
        scratch_shapes=[pltpu.VMEM(a.shape, a.dtype) for a in operands]
        + [
            pltpu.VMEM((lines, 128), jnp.int32),
        ]
        + [pltpu.SMEM((4, 128), jnp.int32)] * 4
        + [
            pltpu.SemaphoreType.DMA((8,)),
            pltpu.SemaphoreType.DMA((4,)),
            pltpu.VMEM((cols, 128), F32),
            pltpu.VMEM((ndose * nclip, width), F32),
            pltpu.VMEM((cols, width), F32),
            pltpu.VMEM((2, 2 * width, width), F32),
            pltpu.VMEM((lines * 128, width), F32),
            pltpu.SemaphoreType.DMA((4,)),
        ],
        compiler_params=pltpu.CompilerParams(vmem_limit_bytes=56 * 2**20),
        name="compute",
    )(*operands)


def shards(clip_cache, dose_scale, focus_term, clip_ids, dose_ids, focus_ids):
    rows = clip_ids.shape[0]
    ids = [a.reshape(rows // 128, 128) for a in (clip_ids, dose_ids, focus_ids)]
    gathered = call_exchange(lax.axis_size("panel"), clip_cache, dose_scale, focus_term, ids)
    return call_compute(rows * lax.axis_size("slab"), *gathered, ids)


def solution(mesh):
    return jax.shard_map(
        shards,
        mesh=mesh,
        in_specs=(
            P(None, "panel"),
            P(None, "panel"),
            P(None, "panel"),
            P("slab"),
            P("slab"),
            P("slab"),
        ),
        out_specs=P("slab", "panel"),
        check_vma=False,
    )
```
